256 devices in a mesh: section: 16 (over z_hi, x, core), dp: 16 (over z_lo, y).
Axes of the slice: x: 4, y: 4, z: 8 (z_hi: 2, z_lo: 4; z = z_hi * 4 + z_lo), core: 2. Of those that a mesh axis runs over, the one named last changes fastest.
Arguments:
- inputs: bfloat16 [3, 1024, 3072], P(None, 'dp'), may hold values from -6 to 6
- cotangent: bfloat16 [3, 1024, 3072], P(None, 'dp'), may hold values from -6 to 6
- weight: bfloat16 [16, 3072, 3072], P('section', 'dp'), may hold values from -0.109375 to 0.109375
- gain: float32 [16, 3072], replicated, may hold values from 0.25 to 1.75
Outputs:
- weight_grad: bfloat16 [16, 3072, 3072], P('section', 'dp')
- gain_grad: float32 [16, 3072], P('section')
- input_grad: bfloat16 [3, 1024, 3072], P(None, 'dp', 'section')
- final_hidden: bfloat16 [3, 1024, 3072], P(None, 'dp', 'section')
The draws below stay inside these ranges and needn't reach their ends.
All inputs are finite; a program needn't handle non-finite values.
Results may differ from the reference program's by a relative error of at most 0.035.
Values may be sent and summed in bfloat16 or wider, within the bound.
No kernel may reach another device: no remote copies, remote signals or barrier semaphores. Data moves between devices by JAX's collectives and lax.ppermute only.
A program may use at most 128 MiB of HBM per device.

```python
import jax
import jax.numpy as jnp
from jax import lax

DW = 3072
MB = 3
TOK_MB = 64
LAYERS = 16
TOKENS = 1024
N_DP = 16


def block_scale(key, shape, cuts, smallest, top_value):
    level, own = 1.0, jax.random.fold_in(key, 6)
    for dim, blocks in cuts:
        draws = jnp.exp(jax.random.uniform(jax.random.fold_in(own, dim), (blocks,), jnp.float32, smallest / len(cuts), top_value / len(cuts)))
        level = level * jnp.repeat(draws, shape[dim] // blocks).reshape([-1 if axis == dim else 1 for axis in range(len(shape))])
    return level


def noise(rng, dims, spread, most, shards=(), held_as=jnp.bfloat16):
    entries = spread * jax.random.normal(rng, dims, jnp.float32)
    if shards:
        entries = entries * block_scale(rng, dims, shards, -0.22, 0.18)
    return jnp.clip(entries, -most, most).astype(held_as)


def setup_inputs(seed: int = 0) -> dict:
    keys = jax.random.split(jax.random.key(seed), 5)
    return {
        "inputs": noise(keys[0], (MB, TOKENS, DW), 1.0, 6.0, ((1, 16),)),
        "cotangent": noise(keys[1], (MB, TOKENS, DW), 1.0, 6.0, ((1, 16),)),
        "weight": noise(keys[2], (LAYERS, DW, DW), DW ** -0.5, 0.109375, ((0, 16), (1, 16))),
        "gain": jnp.clip(1.0 + 0.15 * jax.random.normal(keys[3], (LAYERS, DW), jnp.float32), 0.25, 1.75),
    }


EPSILON = 1e-06
HALF_ROOT = 0.7071067811865476
DENSITY = 0.3989422804014327

def normalize(hidden):
    values = hidden.astype(jnp.float32)
    scale = lax.rsqrt(lax.optimization_barrier(jnp.mean(values * values, axis=-1, keepdims=True)) + EPSILON)
    return (values, scale, values * scale)

def gelu_value(pre):
    return 0.5 * pre * (1.0 + jax.scipy.special.erf(pre * HALF_ROOT))

def gelu_slope(pre):
    return 0.5 * (1.0 + jax.scipy.special.erf(pre * HALF_ROOT)) + pre * jnp.exp(-0.5 * pre * pre) * DENSITY

def layer_forward(hidden, gain_row, matrix):
    values, scale, unit = normalize(hidden)
    normed = (unit * gain_row).astype(jnp.bfloat16)
    pre = jnp.dot(normed, matrix, preferred_element_type=jnp.float32)
    return ((values + gelu_value(pre)).astype(jnp.bfloat16), pre)

def layer_backward(upstream, hidden, pre, gain_row, matrix):
    values, scale, unit = normalize(hidden)
    normed = (unit * gain_row).astype(jnp.bfloat16)
    arriving = upstream.astype(jnp.float32)
    slope = (arriving * gelu_slope(pre)).astype(jnp.bfloat16)
    normed_grad = lax.dot_general(slope, matrix, (((1,), (1,)), ((), ())), preferred_element_type=jnp.float32)
    gain_term = lax.optimization_barrier(jnp.sum(normed_grad * unit, axis=0))
    unit_grad = normed_grad * gain_row
    centred = unit_grad - unit * lax.optimization_barrier(jnp.mean(unit_grad * unit, axis=-1, keepdims=True))
    downstream = (arriving + scale * centred).astype(jnp.bfloat16)
    return (downstream, normed, slope, gain_term)

def reference(inputs, cotangent, weight, gain):
    micro_count = inputs.shape[0]

    def forward(hidden, layer):
        matrix, gain_row = layer
        result, pre = layer_forward(hidden, gain_row, matrix)
        return (result, (hidden, pre))
    last_hidden, saved = lax.scan(forward, inputs.reshape(-1, DW), (weight, gain))
    hiddens, pres = saved

    def group_rows(table):
        shaped = table.reshape(micro_count, N_DP, TOK_MB, DW)
        return shaped.transpose(1, 0, 2, 3).reshape(N_DP, micro_count * TOK_MB, DW)

    def accumulate(total, pair):
        left, right = pair
        part = lax.dot_general(left, right, (((0,), (0,)), ((), ())), preferred_element_type=jnp.float32)
        return (total + part.astype(jnp.bfloat16).astype(jnp.float32), None)

    def backward(upstream, layer):
        matrix, gain_row, hidden, pre = layer
        downstream, normed, slope, gain_term = layer_backward(upstream, hidden, pre, gain_row, matrix)
        start_total = jnp.zeros((DW, DW), jnp.float32)
        total, _ = lax.scan(accumulate, start_total, (group_rows(normed), group_rows(slope)))
        return (downstream, (total.astype(jnp.bfloat16), gain_term))
    first_grad, grads = lax.scan(backward, cotangent.reshape(-1, DW), (weight, gain, hiddens, pres), reverse=True)
    weight_grads, gain_grads = grads
    return (weight_grads, gain_grads, first_grad.reshape(inputs.shape), last_hidden.reshape(inputs.shape))
```

```python
import functools

import jax
import jax.numpy as jnp
from jax import lax
from jax.experimental import pallas as pl
from jax.experimental.pallas import tpu as pltpu
from jax.sharding import PartitionSpec as P

EPSILON = 1e-06
HALF_ROOT = 0.7071067811865476
DENSITY = 0.3989422804014327
BF = jnp.bfloat16
F32 = jnp.float32
ANY = pl.BlockSpec(memory_space=pl.ANY)
HBM = pl.BlockSpec(memory_space=pltpu.HBM)
VMEM = pl.BlockSpec(memory_space=pltpu.VMEM)
SMEM = pl.BlockSpec(memory_space=pltpu.SMEM)
TILE = 512
LIMIT = 8 * 1024 * 1024


def call(kernel, outs, in_specs, out_specs, aliases, scratch, operands):
    return pl.pallas_call(
        kernel,
        out_shape=outs,
        in_specs=in_specs,
        out_specs=out_specs,
        input_output_aliases=aliases,
        scratch_shapes=scratch,
        compiler_params=pltpu.CompilerParams(vmem_limit_bytes=LIMIT),
    )(*operands)


def hold_kernel(source, held, sem):
    copy = pltpu.make_async_copy(source, held, sem)
    copy.start()
    copy.wait()


def hold(matrix):
    shape = pltpu.VMEM(matrix.shape, matrix.dtype)
    return call(
        hold_kernel, shape, [ANY], VMEM, {}, [pltpu.SemaphoreType.DMA], [matrix]
    )


def turn_kernel(source, turned):
    for i in range(0, source.shape[0], TILE):
        for j in range(0, source.shape[1], TILE):
            turned[pl.ds(j, TILE), pl.ds(i, TILE)] = source[pl.ds(i, TILE), pl.ds(j, TILE)].T


def turn(matrix):
    shape = pltpu.VMEM(matrix.shape, matrix.dtype)
    return call(turn_kernel, shape, [VMEM], VMEM, {}, [], [matrix])


def unit_of(values):
    scale = lax.rsqrt(jnp.mean(values * values, axis=-1, keepdims=True) + EPSILON)
    return scale, values * scale


def forward_kernel(t, m, section, x_in, gain, matrix, *refs):
    y, saved_out, normed_out, factor_out, saved, normed, factor, sems = refs[-8:]

    @pl.when(section[0] == t)
    def _():
        x = x_in.at[m] if m is not None else x_in
        saved[...] = x[...]
        keep = [pltpu.make_async_copy(saved, saved_out, sems.at[0])]
        keep[-1].start()
        _, unit = unit_of(saved[...].astype(F32))
        normed[...] = (unit * gain[...]).astype(BF)
        keep.append(pltpu.make_async_copy(normed, normed_out, sems.at[1]))
        keep[-1].start()
        for n in range(saved.shape[1] // TILE):
            at = pl.ds(n * TILE, TILE)
            pre = jnp.dot(normed[...], matrix[:, at], preferred_element_type=F32)
            bell = 0.5 * (1.0 + lax.erf(pre * HALF_ROOT))
            y[:, at] = (saved[:, at].astype(F32) + pre * bell).astype(BF)
            factor[:, at] = bell + pre * jnp.exp(-0.5 * pre * pre) * DENSITY
            copy = pltpu.make_async_copy(factor.at[:, at], factor_out.at[:, at], sems.at[2 + n])
            copy.start()
            keep.append(copy)
        for copy in keep:
            copy.wait()


def forward(t, m, section, x, gain_row, matrix, kept):
    shape = x.shape[-2:]
    wide, deep = pltpu.HBM(shape, BF), pltpu.HBM(shape, F32)
    return call(
        functools.partial(forward_kernel, t, m if x.ndim == 3 else None),
        (pltpu.VMEM(shape, BF), wide, wide, deep),
        [SMEM] + [VMEM] * 3 + [HBM] * len(kept),
        (VMEM, HBM, HBM, HBM),
        {4 + i: 1 + i for i in range(len(kept))},
        [
            pltpu.VMEM(shape, BF),
            pltpu.VMEM(shape, BF),
            pltpu.VMEM(shape, F32),
            pltpu.SemaphoreType.DMA((2 + shape[1] // TILE,)),
        ],
        [section, x, gain_row, matrix, *kept],
    )


def backward_kernel(t, m, section, u_in, saved, factor, gain, turned, *refs):
    d, slope_out, term_out, slope, term, grad, sems = refs[-7:]

    @pl.when(section[0] == t)
    def _():
        u = u_in.at[m] if m is not None else u_in
        slope[...] = (u[...].astype(F32) * factor[...]).astype(BF)
        keep_slope = pltpu.make_async_copy(slope, slope_out, sems.at[0])
        keep_slope.start()
        for k in range(0, saved.shape[1], TILE):
            at = pl.ds(k, TILE)
            grad[:, at] = jnp.dot(slope[...], turned[:, at], preferred_element_type=F32)
        scale, unit = unit_of(saved[...].astype(F32))
        normed_grad = grad[...]
        term[...] = jnp.sum(normed_grad * unit, axis=0, keepdims=True)
        keep_term = pltpu.make_async_copy(term, term_out, sems.at[1])
        keep_term.start()
        unit_grad = normed_grad * gain[...]
        centred = unit_grad - unit * jnp.mean(unit_grad * unit, axis=-1, keepdims=True)
        d[...] = (u[...].astype(F32) + scale * centred).astype(BF)
        keep_slope.wait()
        keep_term.wait()


def backward(t, m, section, u, saved, factor, gain_row, turned, kept):
    shape = saved.shape
    return call(
        functools.partial(backward_kernel, t, m if u.ndim == 3 else None),
        (
            pltpu.VMEM(shape, BF),
            pltpu.HBM(shape, BF),
            pltpu.HBM((1, shape[1]), F32),
        ),
        [SMEM] + [VMEM] * 5 + [HBM] * len(kept),
        (VMEM, HBM, HBM),
        {6 + i: 1 + i for i in range(len(kept))},
        [
            pltpu.VMEM(shape, BF),
            pltpu.VMEM((1, shape[1]), F32),
            pltpu.VMEM(shape, F32),
            pltpu.SemaphoreType.DMA((2,)),
        ],
        [section, u, saved, factor, gain_row, turned, *kept],
    )


def mirrored(index, count):
    return count - 4 - index // 4 * 4 + index % 4


def hop(block, source, target, half, count):
    crosses = (source < half) != (target < half)
    route = [
        (source * count + i, target * count + (mirrored(i, count) if crosses else i))
        for i in range(count)
    ]
    return lax.ppermute(block, ("section", "dp"), route)


def spread(block, owner, sections, count, turn):
    share = block.shape[1] // sections
    total = None
    for s in range(sections):
        route = [
            (owner * count + (mirrored(i, count) if turn else i), s * count + i)
            for i in range(count)
        ]
        piece = block[:, s * share : (s + 1) * share]
        part = lax.ppermute(piece, ("section", "dp"), route)
        total = part if total is None else total + part
    return total


def on_device(inputs, cotangent, weight, gain):
    sections = lax.axis_size("section")
    count = lax.axis_size("dp")
    half = sections // 2
    section = lax.axis_index("section")
    micros, rows, features = inputs.shape
    here = section.astype(jnp.int32).reshape(1)
    gain_row = lax.dynamic_index_in_dim(gain, section, 0, keepdims=True)
    across = [(i, mirrored(i, count)) for i in range(count)]
    upstream = lax.ppermute(cotangent, "dp", across)
    gathered = lax.all_gather(weight[0], "dp", axis=0, tiled=True)
    gathered, upstream, inputs, gain_row, here = lax.optimization_barrier(
        (gathered, upstream, inputs, gain_row, here)
    )
    matrix = hold(gathered)

    kept = [()] * micros
    current = [inputs] * micros
    for t in range(sections):
        if t == half:
            turned = turn(matrix)
        for m in range(micros):
            result, *kept[m] = forward(t, m, here, current[m], gain_row, matrix, kept[m])
            current[m] = hop(result, t, t + 1, half, count) if t + 1 < sections else result
    last = current

    passed = [()] * micros
    arriving = [upstream] * micros
    for t in reversed(range(sections)):
        for m in range(micros):
            saved, _, factor = kept[m]
            result, *passed[m] = backward(
                t, m, here, arriving[m], saved, factor, gain_row, turned, passed[m]
            )
            arriving[m] = hop(result, t, t - 1, half, count) if t else result
    slope = [passed[m][0] for m in range(micros)]
    total = sum(passed[m][1] for m in range(micros))
    normed = [kept[m][1] for m in range(micros)]
    last, first = jnp.concatenate(last, axis=0), jnp.concatenate(arriving, axis=0)

    summed = lax.psum_scatter(
        lax.dot_general(
            jnp.concatenate(normed, axis=0), jnp.concatenate(slope, axis=0),
            (((0,), (0,)), ((), ())), preferred_element_type=F32,
        ).astype(BF),
        "dp",
        scatter_dimension=0,
        tiled=True,
    )
    gain_grad = lax.psum(total, "dp")
    final_share = spread(last, sections - 1, sections, count, True)
    first_share = spread(first, 0, sections, count, False)
    shape = (micros, rows, features // sections)
    return (
        summed[None],
        gain_grad,
        first_share.reshape(shape),
        final_share.reshape(shape),
    )


def solution(mesh):
    in_specs = (P(None, "dp", None), P(None, "dp", None), P("section", "dp", None), P())
    out_specs = (
        P("section", "dp", None),
        P("section", None),
        P(None, "dp", "section"),
        P(None, "dp", "section"),
    )
    return jax.shard_map(
        on_device, mesh=mesh, in_specs=in_specs, out_specs=out_specs, check_vma=False
    )
```

```python
import functools

import jax
import jax.numpy as jnp
from jax import lax
from jax.experimental import pallas as pl
from jax.experimental.pallas import tpu as pltpu
from jax.sharding import PartitionSpec as P

EPSILON = 1e-06
HALF_ROOT = 0.7071067811865476
DENSITY = 0.3989422804014327
BF = jnp.bfloat16
F32 = jnp.float32
ANY = pl.BlockSpec(memory_space=pl.ANY)
HBM = pl.BlockSpec(memory_space=pltpu.HBM)
VMEM = pl.BlockSpec(memory_space=pltpu.VMEM)
SMEM = pl.BlockSpec(memory_space=pltpu.SMEM)
TILE = 512
LIMIT = 8 * 1024 * 1024


def call(kernel, outs, in_specs, out_specs, aliases, scratch, operands):
    return pl.pallas_call(
        kernel,
        out_shape=outs,
        in_specs=in_specs,
        out_specs=out_specs,
        input_output_aliases=aliases,
        scratch_shapes=scratch,
        compiler_params=pltpu.CompilerParams(vmem_limit_bytes=LIMIT),
    )(*operands)


def hold_kernel(source, held, sem):
    copy = pltpu.make_async_copy(source, held, sem)
    copy.start()
    copy.wait()


def hold(matrix):
    shape = pltpu.VMEM(matrix.shape, matrix.dtype)
    return call(
        hold_kernel, shape, [ANY], VMEM, {}, [pltpu.SemaphoreType.DMA], [matrix]
    )


def turn_kernel(source, turned):
    for i in range(0, source.shape[0], TILE):
        for j in range(0, source.shape[1], TILE):
            turned[pl.ds(j, TILE), pl.ds(i, TILE)] = source[pl.ds(i, TILE), pl.ds(j, TILE)].T


def turn(matrix):
    shape = pltpu.VMEM(matrix.shape, matrix.dtype)
    return call(turn_kernel, shape, [VMEM], VMEM, {}, [], [matrix])


def unit_of(values):
    scale = lax.rsqrt(jnp.mean(values * values, axis=-1, keepdims=True) + EPSILON)
    return scale, values * scale


def forward_kernel(t, m, section, x_in, gain, matrix, *refs):
    y, saved_out, normed_out, factor_out, saved, normed, factor, sems = refs[-8:]

    @pl.when(section[0] == t)
    def _():
        x = x_in.at[m] if m is not None else x_in
        saved[...] = x[...]
        keep = [pltpu.make_async_copy(saved, saved_out, sems.at[0])]
        keep[-1].start()
        _, unit = unit_of(saved[...].astype(F32))
        normed[...] = (unit * gain[...]).astype(BF)
        keep.append(pltpu.make_async_copy(normed, normed_out, sems.at[1]))
        keep[-1].start()
        for n in range(saved.shape[1] // TILE):
            at = pl.ds(n * TILE, TILE)
            pre = jnp.dot(normed[...], matrix[:, at], preferred_element_type=F32)
            bell = 0.5 * (1.0 + lax.erf(pre * HALF_ROOT))
            y[:, at] = (saved[:, at].astype(F32) + pre * bell).astype(BF)
            factor[:, at] = bell + pre * jnp.exp(-0.5 * pre * pre) * DENSITY
            copy = pltpu.make_async_copy(factor.at[:, at], factor_out.at[:, at], sems.at[2 + n])
            copy.start()
            keep.append(copy)
        for copy in keep:
            copy.wait()


def forward(t, m, section, x, gain_row, matrix, kept):
    shape = x.shape[-2:]
    wide, deep = pltpu.HBM(shape, BF), pltpu.HBM(shape, F32)
    return call(
        functools.partial(forward_kernel, t, m if x.ndim == 3 else None),
        (pltpu.VMEM(shape, BF), wide, wide, deep),
        [SMEM] + [VMEM] * 3 + [HBM] * len(kept),
        (VMEM, HBM, HBM, HBM),
        {4 + i: 1 + i for i in range(len(kept))},
        [
            pltpu.VMEM(shape, BF),
            pltpu.VMEM(shape, BF),
            pltpu.VMEM(shape, F32),
            pltpu.SemaphoreType.DMA((2 + shape[1] // TILE,)),
        ],
        [section, x, gain_row, matrix, *kept],
    )


def backward_kernel(t, m, section, u_in, saved, factor, gain, turned, *refs):
    d, slope_out, term_out, slope, term, grad, sems = refs[-7:]

    @pl.when(section[0] == t)
    def _():
        u = u_in.at[m] if m is not None else u_in
        slope[...] = (u[...].astype(F32) * factor[...]).astype(BF)
        keep_slope = pltpu.make_async_copy(slope, slope_out, sems.at[0])
        keep_slope.start()
        for k in range(0, saved.shape[1], TILE):
            at = pl.ds(k, TILE)
            grad[:, at] = jnp.dot(slope[...], turned[:, at], preferred_element_type=F32)
        scale, unit = unit_of(saved[...].astype(F32))
        normed_grad = grad[...]
        term[...] = jnp.sum(normed_grad * unit, axis=0, keepdims=True)
        keep_term = pltpu.make_async_copy(term, term_out, sems.at[1])
        keep_term.start()
        unit_grad = normed_grad * gain[...]
        centred = unit_grad - unit * jnp.mean(unit_grad * unit, axis=-1, keepdims=True)
        d[...] = (u[...].astype(F32) + scale * centred).astype(BF)
        keep_slope.wait()
        keep_term.wait()


def backward(t, m, section, u, saved, factor, gain_row, turned, kept):
    shape = saved.shape
    return call(
        functools.partial(backward_kernel, t, m if u.ndim == 3 else None),
        (
            pltpu.VMEM(shape, BF),
            pltpu.HBM(shape, BF),
            pltpu.HBM((1, shape[1]), F32),
        ),
        [SMEM] + [VMEM] * 5 + [HBM] * len(kept),
        (VMEM, HBM, HBM),
        {6 + i: 1 + i for i in range(len(kept))},
        [
            pltpu.VMEM(shape, BF),
            pltpu.VMEM((1, shape[1]), F32),
            pltpu.VMEM(shape, F32),
            pltpu.SemaphoreType.DMA((2,)),
        ],
        [section, u, saved, factor, gain_row, turned, *kept],
    )


def mirrored(index, count):
    return count - 4 - index // 4 * 4 + index % 4


def hop(block, lower, half, count):
    if lower == half - 1:
        lowers = [lower]
    elif lower % 2:
        lowers = [s for s in range(1, 2 * half - 1, 2) if s != half - 1]
    else:
        lowers = list(range(0, 2 * half, 2))
    pairs = []
    for s in lowers:
        for i in range(count):
            j = mirrored(i, count) if s == half - 1 else i
            near, far = s * count + i, (s + 1) * count + j
            pairs += [(near, far), (far, near)]
    return lax.ppermute(block, ("section", "dp"), sorted(pairs))


def shares(blocks, sections):
    cut = jnp.stack([block.reshape(block.shape[0], sections, -1) for block in blocks])
    return lax.all_to_all(cut, "section", split_axis=2, concat_axis=2)


def on_device(inputs, cotangent, weight, gain):
    sections = lax.axis_size("section")
    count = lax.axis_size("dp")
    half = sections // 2
    section = lax.axis_index("section")
    micros, rows, features = inputs.shape
    here = section.astype(jnp.int32).reshape(1)
    gain_row = lax.dynamic_index_in_dim(gain, section, 0, keepdims=True)
    across = [(i, mirrored(i, count)) for i in range(count)]
    gathered = lax.all_gather(weight[0], "dp", axis=0, tiled=True)
    gathered, cotangent, inputs, gain_row, here = lax.optimization_barrier(
        (gathered, cotangent, inputs, gain_row, here)
    )
    matrix = hold(gathered)
    upstream = lax.ppermute(cotangent, "dp", across)

    kept = [()] * micros
    current = [inputs] * micros
    for t in range(sections):
        if t == half:
            turned = turn(matrix)
        for m in range(micros):
            result, *kept[m] = forward(t, m, here, current[m], gain_row, matrix, kept[m])
            current[m] = hop(result, t, half, count) if t + 1 < sections else result
    last = current

    passed = [()] * micros
    arriving = [upstream] * micros
    for t in reversed(range(sections)):
        for m in range(micros):
            saved, _, factor = kept[m]
            result, *passed[m] = backward(
                t, m, here, arriving[m], saved, factor, gain_row, turned, passed[m]
            )
            arriving[m] = hop(result, t - 1, half, count) if t else result
    slope = [passed[m][0] for m in range(micros)]
    total = sum(passed[m][1] for m in range(micros))
    normed = [kept[m][1] for m in range(micros)]
    last, first = jnp.concatenate(last, axis=0), jnp.concatenate(arriving, axis=0)

    summed = lax.psum_scatter(
        lax.dot_general(
            jnp.concatenate(normed, axis=0), jnp.concatenate(slope, axis=0),
            (((0,), (0,)), ((), ())), preferred_element_type=F32,
        ).astype(BF),
        "dp",
        scatter_dimension=0,
        tiled=True,
    )
    gain_grad = lax.psum(total, "dp")
    shared = shares((first, last), sections)
    first_share = shared[0, :, 0]
    final_share = lax.ppermute(shared[1, :, sections - 1], "dp", across)
    shape = (micros, rows, features // sections)
    return (
        summed[None],
        gain_grad,
        first_share.reshape(shape),
        final_share.reshape(shape),
    )


def solution(mesh):
    in_specs = (P(None, "dp", None), P(None, "dp", None), P("section", "dp", None), P())
    out_specs = (
        P("section", "dp", None),
        P("section", None),
        P(None, "dp", "section"),
        P(None, "dp", "section"),
    )
    return jax.shard_map(
        on_device, mesh=mesh, in_specs=in_specs, out_specs=out_specs, check_vma=False
    )
```

```python
import functools

import jax
import jax.numpy as jnp
import numpy as np
from jax import lax
from jax.experimental import pallas as pl
from jax.experimental.pallas import tpu as pltpu
from jax.sharding import PartitionSpec as P

EPSILON = 1e-06
HALF_ROOT = 0.7071067811865476
DENSITY = 0.3989422804014327
BF = jnp.bfloat16
F32 = jnp.float32
ANY = pl.BlockSpec(memory_space=pl.ANY)
HBM = pl.BlockSpec(memory_space=pltpu.HBM)
VMEM = pl.BlockSpec(memory_space=pltpu.VMEM)
SMEM = pl.BlockSpec(memory_space=pltpu.SMEM)
TILE = 512
LIMIT = 8 * 1024 * 1024


def call(kernel, outs, in_specs, out_specs, aliases, scratch, operands):
    return pl.pallas_call(
        kernel,
        out_shape=outs,
        in_specs=in_specs,
        out_specs=out_specs,
        input_output_aliases=aliases,
        scratch_shapes=scratch,
        compiler_params=pltpu.CompilerParams(vmem_limit_bytes=LIMIT),
    )(*operands)


def hold_kernel(source, held, sem):
    copy = pltpu.make_async_copy(source, held, sem)
    copy.start()
    copy.wait()


def hold(matrix):
    shape = pltpu.VMEM(matrix.shape, matrix.dtype)
    return call(
        hold_kernel, shape, [ANY], VMEM, {}, [pltpu.SemaphoreType.DMA], [matrix]
    )


def turn_kernel(source, turned):
    for i in range(0, source.shape[0], TILE):
        for j in range(0, source.shape[1], TILE):
            turned[pl.ds(j, TILE), pl.ds(i, TILE)] = source[pl.ds(i, TILE), pl.ds(j, TILE)].T


def turn(matrix):
    shape = pltpu.VMEM(matrix.shape, matrix.dtype)
    return call(turn_kernel, shape, [VMEM], VMEM, {}, [], [matrix])


def in_hbm(array):
    return pltpu.with_memory_space_constraint(array, pltpu.HBM)


def unit_of(values):
    scale = lax.rsqrt(jnp.mean(values * values, axis=-1, keepdims=True) + EPSILON)
    return scale, values * scale


def forward_kernel(t, m, section, x_in, gain, matrix, *refs):
    y, saved_out, normed_out, factor_out, saved, normed, factor, sems = refs[-8:]

    @pl.when(section[0] == t)
    def _():
        x = x_in.at[m] if m is not None else x_in
        saved[...] = x[...]
        keep = [pltpu.make_async_copy(saved, saved_out, sems.at[0])]
        keep[-1].start()
        _, unit = unit_of(saved[...].astype(F32))
        normed[...] = (unit * gain[...]).astype(BF)
        keep.append(pltpu.make_async_copy(normed, normed_out, sems.at[1]))
        keep[-1].start()
        for n in range(saved.shape[1] // TILE):
            at = pl.ds(n * TILE, TILE)
            pre = jnp.dot(normed[...], matrix[:, at], preferred_element_type=F32)
            bell = 0.5 * (1.0 + lax.erf(pre * HALF_ROOT))
            y[:, at] = (saved[:, at].astype(F32) + pre * bell).astype(BF)
            factor[:, at] = bell + pre * jnp.exp(-0.5 * pre * pre) * DENSITY
            copy = pltpu.make_async_copy(factor.at[:, at], factor_out.at[:, at], sems.at[2 + n])
            copy.start()
            keep.append(copy)
        for copy in keep:
            copy.wait()


def forward(t, m, section, x, gain_row, matrix, kept, after):
    shape = x.shape[-2:]
    wide, deep = pltpu.HBM(shape, BF), pltpu.HBM(shape, F32)
    return call(
        functools.partial(forward_kernel, t, m if x.ndim == 3 else None),
        (pltpu.VMEM(shape, BF), wide, wide, deep),
        [SMEM] + [VMEM] * 3 + [HBM] * (len(kept) + len(after)),
        (VMEM, HBM, HBM, HBM),
        {4 + i: 1 + i for i in range(len(kept))},
        [
            pltpu.VMEM(shape, BF),
            pltpu.VMEM(shape, BF),
            pltpu.VMEM(shape, F32),
            pltpu.SemaphoreType.DMA((2 + shape[1] // TILE,)),
        ],
        [section, x, gain_row, matrix, *kept, *after],
    )


def backward_kernel(t, m, pins, section, u_in, saved, factor, gain, turned, *refs):
    slope, term, grad, sems = refs[-4:]
    d, slope_out, term_out = refs[-7 - pins : len(refs) - 4 - pins]

    @pl.when(section[0] == t)
    def _():
        u = u_in.at[m] if m is not None else u_in
        slope[...] = (u[...].astype(F32) * factor[...]).astype(BF)
        keep_slope = pltpu.make_async_copy(slope, slope_out, sems.at[0])
        keep_slope.start()
        for k in range(0, saved.shape[1], TILE):
            at = pl.ds(k, TILE)
            grad[:, at] = jnp.dot(slope[...], turned[:, at], preferred_element_type=F32)
        scale, unit = unit_of(saved[...].astype(F32))
        normed_grad = grad[...]
        term[...] = jnp.sum(normed_grad * unit, axis=0, keepdims=True)
        keep_term = pltpu.make_async_copy(term, term_out, sems.at[1])
        keep_term.start()
        unit_grad = normed_grad * gain[...]
        centred = unit_grad - unit * jnp.mean(unit_grad * unit, axis=-1, keepdims=True)
        d[...] = (u[...].astype(F32) + scale * centred).astype(BF)
        keep_slope.wait()
        keep_term.wait()


def backward(t, m, section, u, saved, factor, gain_row, turned, kept, after, pinned):
    shape = saved.shape
    first = 6 + len(kept) + len(after)
    aliases = {6 + i: 1 + i for i in range(len(kept))}
    aliases.update({first + i: 3 + i for i in range(len(pinned))})
    return call(
        functools.partial(backward_kernel, t, m if u.ndim == 3 else None, len(pinned)),
        (
            pltpu.VMEM(shape, BF),
            pltpu.HBM(shape, BF),
            pltpu.HBM((1, shape[1]), F32),
            *(pltpu.HBM(p.shape, p.dtype) for p in pinned),
        ),
        [SMEM] + [VMEM] * 5 + [HBM] * (first - 6 + len(pinned)),
        (VMEM,) + (HBM,) * (2 + len(pinned)),
        aliases,
        [
            pltpu.VMEM(shape, BF),
            pltpu.VMEM((1, shape[1]), F32),
            pltpu.VMEM(shape, F32),
            pltpu.SemaphoreType.DMA((2,)),
        ],
        [section, u, saved, factor, gain_row, turned, *kept, *after, *pinned],
    )


def mirrored(index, count):
    return count - 4 - index // 4 * 4 + index % 4


def hop(block, lower, half, count):
    pairs = []
    for t in [lower] if lower == half - 1 else [lower % half, lower % half + half]:
        for i in range(count):
            j = mirrored(i, count) if t == half - 1 else i
            near, far = t * count + i, (t + 1) * count + j
            pairs += [(near, far), (far, near)]
    return lax.ppermute(block, ("section", "dp"), sorted(pairs))


def order(sections, micros):
    steps = [(t, m) for t in range(sections) for m in range(micros)]
    return sorted(steps, key=lambda p: micros * p[0] + (micros - 1) * p[1])


def spread(block, owner, sections, section):
    bit = sections // 2
    while bit:
        width = block.shape[1] // 2
        low, high = block[:, :width], block[:, width:]
        upper = (section & bit) != 0
        pairs = [(s, s ^ bit) for s in range(sections)]
        arrived = lax.ppermute(jnp.where(upper, low, high), "section", pairs)
        block = jnp.where(upper == bool(owner & bit), jnp.where(upper, high, low), arrived)
        bit //= 2
    return block


RING = (0, 2, 3, 1)


def z_after(z, k):
    return RING[(RING.index(z) + k) % len(RING)]


def shift_z(block, k, count):
    pairs = [(i, 4 * z_after(i // 4, k) + i % 4) for i in range(count)]
    return lax.ppermute(block, "dp", pairs)


def shift_y(block, k, count):
    pairs = [(i, i // 4 * 4 + (i + k) % 4) for i in range(count)]
    return lax.ppermute(block, "dp", pairs)


def pick(blocks, at):
    return lax.dynamic_index_in_dim(blocks, at, 0, keepdims=False)


def from_all_y(block, count):
    left, right = shift_y(block, 1, count), shift_y(block, 3, count)
    rows = block.shape[0] // 2
    far = jnp.concatenate(
        [shift_y(left[:rows], 1, count), shift_y(right[rows:], 3, count)], axis=0
    )
    return [block, left, far, right]


def from_all_z(block, count):
    blocks = [block]
    for _ in range(3):
        blocks.append(shift_z(blocks[-1], 1, count))
    return blocks


def on_device(inputs, cotangent, weight, gain):
    sections = lax.axis_size("section")
    count = lax.axis_size("dp")
    half = sections // 2
    section = lax.axis_index("section")
    place = lax.axis_index("dp")
    z, y = place // 4, place % 4
    ahead = jnp.asarray([[z_after(i, k) for i in range(4)] for k in range(4)], jnp.int32)
    behind = jnp.asarray([[z_after(i, -k) for i in range(4)] for k in range(4)], jnp.int32)
    to_z = [ahead[k, z] for k in range(4)]
    from_z = [behind[k, z] for k in range(4)]
    micros, rows, features = inputs.shape
    here = section.astype(jnp.int32).reshape(1)
    gain_row = lax.dynamic_index_in_dim(gain, section, 0, keepdims=True)
    across = [(i, mirrored(i, count)) for i in range(count)]
    gathered = lax.all_gather(weight[0], "dp", axis=0, tiled=True)
    gathered, cotangent, inputs, gain_row, here = lax.optimization_barrier(
        (gathered, cotangent, inputs, gain_row, here)
    )
    matrix = hold(gathered)
    upstream = lax.ppermute(cotangent, "dp", across)

    kept = [()] * micros
    current = [inputs] * micros
    after = ()
    turned = None
    for t, m in order(sections, micros):
        if t == half and turned is None:
            turned = turn(matrix)
        result, *kept[m] = forward(t, m, here, current[m], gain_row, matrix, kept[m], after)
        after = (in_hbm(kept[m][0]),)
        current[m] = hop(result, t, half, count) if t + 1 < sections else result

    passed = [()] * micros
    arriving = [upstream] * micros
    parked = [kept[m][1] for m in range(micros)] + current
    for step, m in order(sections, micros):
        t = sections - 1 - step
        pinned = parked if (t, m) == (sections - 6, micros - 1) else []
        result, *rest = backward(
            t, m, here, arriving[m], kept[m][0], kept[m][2], gain_row, turned,
            passed[m], after, pinned,
        )
        passed[m] = rest[:2]
        after = (in_hbm(passed[m][0]),)
        if pinned:
            parked = rest[2:]
            last = jnp.concatenate(parked[micros:], axis=0)
            final_share = spread(lax.ppermute(last, "dp", across), sections - 1, sections, section)
            normed = jnp.concatenate(parked[:micros], axis=0)
            cut = normed.reshape(micros * rows, 4, 4, -1).transpose(2, 0, 1, 3)
            cut = cut.reshape(4, micros * rows, features // 4)
            normed = [pick(cut, y)]
            normed += [shift_y(pick(cut, (y + k) % 4), k, count) for k in (1, 2, 3)]
            normed = from_all_z(jnp.stack(normed), count)
        arriving[m] = hop(result, t - 1, half, count) if t else result

    slope = jnp.concatenate([passed[m][0] for m in range(micros)], axis=0)
    cut = slope.reshape(micros * rows, 4, features // 4).transpose(1, 0, 2)
    slope = [pick(cut, z)]
    slope += [shift_z(pick(cut, to_z[k]), k, count) for k in (1, 2, 3)]
    slope = from_all_y(jnp.concatenate(slope, axis=0), count)
    slope = jnp.stack(slope).reshape(4, 4, micros * rows, features // 4)
    product = jnp.einsum(
        "jkra,kjrb->ab", jnp.stack(normed), slope, preferred_element_type=F32
    ).astype(BF)
    product = product.reshape(4, features // 16, features // 4)
    weight_grad = jnp.zeros((features // 16, features), BF)
    for k in range(4):
        piece = pick(product, to_z[k])
        piece = shift_z(piece, k, count) if k else piece
        at = from_z[k] * (features // 4)
        weight_grad = lax.dynamic_update_slice_in_dim(weight_grad, piece, at, 1)

    total = sum(passed[m][1] for m in range(micros))
    total = total + (shift_y(total, 1, count) + shift_y(total, 2, count) + shift_y(total, 3, count))
    total = total + (shift_z(total, 1, count) + shift_z(total, 2, count) + shift_z(total, 3, count))
    first_share = spread(jnp.concatenate(arriving, axis=0), 0, sections, section)
    shape = (micros, rows, features // sections)
    return (
        weight_grad[None],
        total,
        first_share.reshape(shape),
        final_share.reshape(shape),
    )


def solution(mesh):
    in_specs = (P(None, "dp", None), P(None, "dp", None), P("section", "dp", None), P())
    out_specs = (
        P("section", "dp", None),
        P("section", None),
        P(None, "dp", "section"),
        P(None, "dp", "section"),
    )
    return jax.shard_map(
        on_device, mesh=mesh, in_specs=in_specs, out_specs=out_specs, check_vma=False
    )
```

```python
import functools

import jax
import jax.numpy as jnp
import numpy as np
from jax import lax
from jax.experimental import pallas as pl
from jax.experimental.pallas import tpu as pltpu
from jax.sharding import PartitionSpec as P

EPSILON = 1e-06
HALF_ROOT = 0.7071067811865476
DENSITY = 0.3989422804014327
BF = jnp.bfloat16
F32 = jnp.float32
ANY = pl.BlockSpec(memory_space=pl.ANY)
HBM = pl.BlockSpec(memory_space=pltpu.HBM)
VMEM = pl.BlockSpec(memory_space=pltpu.VMEM)
SMEM = pl.BlockSpec(memory_space=pltpu.SMEM)
TILE = 512
LIMIT = 8 * 1024 * 1024
EARLY = 10


def call(kernel, outs, in_specs, out_specs, aliases, scratch, operands):
    return pl.pallas_call(
        kernel,
        out_shape=outs,
        in_specs=in_specs,
        out_specs=out_specs,
        input_output_aliases=aliases,
        scratch_shapes=scratch,
        compiler_params=pltpu.CompilerParams(vmem_limit_bytes=LIMIT),
        cost_estimate=pl.CostEstimate(flops=1, bytes_accessed=1, transcendentals=0),
    )(*operands)


def hold_kernel(places, row_of, *refs):
    *pieces, held, sems = refs
    copies = []
    for i, (piece, (slot, start, rows, offset, column)) in enumerate(
        (piece, part) for piece, parts in zip(pieces, places) for part in parts
    ):
        row = pl.multiple_of(row_of[slot], 64) + offset
        copies.append(
            pltpu.make_async_copy(
                piece.at[pl.ds(start, rows), :],
                held.at[pl.ds(row, rows), pl.ds(column, piece.shape[1])],
                sems.at[i],
            )
        )
        copies[-1].start()
    for copy in copies:
        copy.wait()


def hold(pieces, row_of, shape):
    arrays, places = zip(*pieces)
    return call(
        functools.partial(hold_kernel, places),
        pltpu.VMEM(shape, BF),
        [SMEM] + [HBM] * len(arrays),
        VMEM,
        {},
        [pltpu.SemaphoreType.DMA((sum(len(p) for p in places),))],
        [row_of] + [in_hbm(array) for array in arrays],
    )


def turn_kernel(source, turned):
    for i in range(0, source.shape[0], TILE):
        for j in range(0, source.shape[1], TILE):
            turned[pl.ds(j, TILE), pl.ds(i, TILE)] = source[pl.ds(i, TILE), pl.ds(j, TILE)].T


def turn(matrix):
    shape = pltpu.VMEM(matrix.shape, matrix.dtype)
    return call(turn_kernel, shape, [VMEM], VMEM, {}, [], [matrix])


def in_hbm(array):
    return pltpu.with_memory_space_constraint(array, pltpu.HBM)


def unit_of(values):
    scale = lax.rsqrt(jnp.mean(values * values, axis=-1, keepdims=True) + EPSILON)
    return scale, values * scale


def forward_kernel(t, m, section, x_in, gain, matrix, *refs):
    y, saved_out, normed_out, factor_out, saved, normed, factor, sems = refs[-8:]

    @pl.when(section[0] == t)
    def _():
        x = x_in.at[m] if m is not None else x_in
        saved[...] = x[...]
        keep = [pltpu.make_async_copy(saved, saved_out, sems.at[0])]
        keep[-1].start()
        _, unit = unit_of(saved[...].astype(F32))
        normed[...] = (unit * gain[...]).astype(BF)
        keep.append(pltpu.make_async_copy(normed, normed_out, sems.at[1]))
        keep[-1].start()
        for n in range(saved.shape[1] // TILE):
            at = pl.ds(n * TILE, TILE)
            pre = jnp.dot(normed[...], matrix[:, at], preferred_element_type=F32)
            bell = 0.5 * (1.0 + lax.erf(pre * HALF_ROOT))
            y[:, at] = (saved[:, at].astype(F32) + pre * bell).astype(BF)
            factor[:, at] = bell + pre * jnp.exp(-0.5 * pre * pre) * DENSITY
            copy = pltpu.make_async_copy(factor.at[:, at], factor_out.at[:, at], sems.at[2 + n])
            copy.start()
            keep.append(copy)
        for copy in keep:
            copy.wait()


def forward(t, m, section, x, gain_row, matrix, kept, after):
    shape = x.shape[-2:]
    wide, deep = pltpu.HBM(shape, BF), pltpu.HBM(shape, F32)
    return call(
        functools.partial(forward_kernel, t, m if x.ndim == 3 else None),
        (pltpu.VMEM(shape, BF), wide, wide, deep),
        [SMEM] + [VMEM] * 3 + [HBM] * (len(kept) + len(after[:1])) + [VMEM] * len(after[1:]),
        (VMEM, HBM, HBM, HBM),
        {4 + i: 1 + i for i in range(len(kept))},
        [
            pltpu.VMEM(shape, BF),
            pltpu.VMEM(shape, BF),
            pltpu.VMEM(shape, F32),
            pltpu.SemaphoreType.DMA((2 + shape[1] // TILE,)),
        ],
        [section, x, gain_row, matrix, *kept, *after],
    )


def backward_kernel(t, m, section, u_in, saved, factor, gain, turned, *refs):
    d, slope_out, term_out, slope, term, grad, sems = refs[-7:]

    @pl.when(section[0] == t)
    def _():
        u = u_in.at[m] if m is not None else u_in
        slope[...] = (u[...].astype(F32) * factor[...]).astype(BF)
        keep_slope = pltpu.make_async_copy(slope, slope_out, sems.at[0])
        keep_slope.start()
        for k in range(0, saved.shape[1], TILE):
            at = pl.ds(k, TILE)
            grad[:, at] = jnp.dot(slope[...], turned[:, at], preferred_element_type=F32)
        scale, unit = unit_of(saved[...].astype(F32))
        normed_grad = grad[...]
        term[...] = jnp.sum(normed_grad * unit, axis=0, keepdims=True)
        keep_term = pltpu.make_async_copy(term, term_out, sems.at[1])
        keep_term.start()
        unit_grad = normed_grad * gain[...]
        centred = unit_grad - unit * jnp.mean(unit_grad * unit, axis=-1, keepdims=True)
        d[...] = (u[...].astype(F32) + scale * centred).astype(BF)
        keep_slope.wait()
        keep_term.wait()


def backward(t, m, section, u, saved, factor, gain_row, turned, kept, after):
    shape = saved.shape
    return call(
        functools.partial(backward_kernel, t, m if u.ndim == 3 else None),
        (pltpu.VMEM(shape, BF), pltpu.HBM(shape, BF), pltpu.HBM((1, shape[1]), F32)),
        [SMEM] + [VMEM] * 5 + [HBM] * (len(kept) + len(after)),
        (VMEM, HBM, HBM),
        {6 + i: 1 + i for i in range(len(kept))},
        [
            pltpu.VMEM(shape, BF),
            pltpu.VMEM((1, shape[1]), F32),
            pltpu.VMEM(shape, F32),
            pltpu.SemaphoreType.DMA((2,)),
        ],
        [section, u, saved, factor, gain_row, turned, *kept, *after],
    )


def mirrored(index, count):
    return count - 4 - index // 4 * 4 + index % 4


def hop(block, lower, half, count):
    pairs = []
    for t in [lower] if lower == half - 1 else [lower % half, lower % half + half]:
        for i in range(count):
            j = mirrored(i, count) if t == half - 1 else i
            near, far = t * count + i, (t + 1) * count + j
            pairs += [(near, far), (far, near)]
    return lax.ppermute(block, ("section", "dp"), sorted(pairs))


def order(sections, micros):
    steps = [(t, m) for t in range(sections) for m in range(micros)]
    return sorted(steps, key=lambda p: (37 * (p[0] // 2) + 14 * (p[0] % 2) + 16 * p[1]))


def spread(first, last, sections, section):
    block, rows = jnp.concatenate([first, last], axis=0), first.shape[0]
    owned = lax.broadcasted_iota(jnp.int32, (2 * rows, 1), 0) >= rows
    bit = sections // 2
    while bit:
        width = block.shape[1] // 2
        low, high = block[:, :width], block[:, width:]
        upper = (section & bit) != 0
        pairs = [(s, s ^ bit) for s in range(sections)]
        arrived = lax.ppermute(jnp.where(upper, low, high), "section", pairs)
        block = jnp.where(owned == upper, jnp.where(upper, high, low), arrived)
        bit //= 2
    return block[:rows], block[rows:]


def cut_kernel(low, high, here, *refs):
    first, second, third, *out, whole, cut, sems = refs

    @pl.when((here[0] >= low) & (here[0] < high))
    def _():
        rows = first.shape[0]
        loads = [
            pltpu.make_async_copy(part, whole.at[pl.ds(i * rows, rows), :], sems.at[i])
            for i, part in enumerate((first, second, third))
        ]
        for load in loads:
            load.start()
        for load in loads:
            load.wait()
        width = whole.shape[1] // 16
        for y in range(4):

            @pl.when(here[1] == y)
            def _():
                for k in range(4):
                    for z in range(4):
                        column = (4 * z + (y + k) % 4) * width
                        cut[k, :, pl.ds(z * width, width)] = whole[:, pl.ds(column, width)]

        stores = [pltpu.make_async_copy(cut.at[k], out[k], sems.at[k]) for k in range(4)]
        for store in stores:
            store.start()
        for store in stores:
            store.wait()


def cut_columns(parts, here, low, high):
    rows, features = 3 * parts[0].shape[0], parts[0].shape[1]
    return call(
        functools.partial(cut_kernel, low, high),
        tuple(pltpu.HBM((rows, features // 4), BF) for _ in range(4)),
        [SMEM] + [HBM] * 3,
        (HBM,) * 4,
        {},
        [
            pltpu.VMEM((rows, features), BF),
            pltpu.VMEM((4, rows, features // 4), BF),
            pltpu.SemaphoreType.DMA((4,)),
        ],
        [here, *(in_hbm(part) for part in parts)],
    )


def pile_kernel(low, high, here, *refs):
    *parts, out, sems = refs

    @pl.when((here[0] >= low) & (here[0] < high))
    def _():
        copies = [
            pltpu.make_async_copy(part, out.at[k], sems.at[k]) for k, part in enumerate(parts)
        ]
        for copy in copies:
            copy.start()
        for copy in copies:
            copy.wait()


def pile(parts, here, low, high):
    return call(
        functools.partial(pile_kernel, low, high),
        pltpu.HBM((len(parts), *parts[0].shape), BF),
        [SMEM] + [HBM] * len(parts),
        HBM,
        {},
        [pltpu.SemaphoreType.DMA((len(parts),))],
        [here, *(in_hbm(part) for part in parts)],
    )


def exchange(parts, here, low, high, count):
    sections = range(low, high)
    cut = cut_columns(parts, here, low, high)
    pieces = [cut[0]]
    for k in (1, 2, 3):
        pairs = [(s * count + i, s * count + i // 4 * 4 + (i + k) % 4) for s in sections for i in range(count)]
        pieces.append(lax.ppermute(cut[k], ("section", "dp"), pairs))
    blocks = [pile(pieces, here, low, high)]
    pairs = [(s * count + i, s * count + 4 * z_after(i // 4, 1) + i % 4) for s in sections for i in range(count)]
    for _ in range(3):
        blocks.append(lax.ppermute(blocks[-1], ("section", "dp"), pairs))
    return blocks


RING = (0, 2, 3, 1)


def z_after(z, k):
    return RING[(RING.index(z) + k) % len(RING)]


def shift_z(block, k, count):
    pairs = [(i, 4 * z_after(i // 4, k) + i % 4) for i in range(count)]
    return lax.ppermute(block, "dp", pairs)


def shift_y(block, k, count):
    pairs = [(i, i // 4 * 4 + (i + k) % 4) for i in range(count)]
    return lax.ppermute(block, "dp", pairs)


def pick(blocks, at):
    return lax.dynamic_index_in_dim(blocks, at, 0, keepdims=False)


def from_all_y(block, count):
    left, right = shift_y(block, 1, count), shift_y(block, 3, count)
    rows = block.shape[0] // 2
    far = jnp.concatenate(
        [shift_y(left[:rows], 1, count), shift_y(right[rows:], 3, count)], axis=0
    )
    return [block, left, far, right]


def from_all_z(block, count):
    blocks = [block]
    for _ in range(3):
        blocks.append(shift_z(blocks[-1], 1, count))
    return blocks


def gather(shard, count):
    rows, features = shard.shape
    part, border = rows // 2, features * 3 // 4
    pieces = []
    first, second = shard[:, :border], shard[:, border:]
    left, right = shift_y(second, 1, count), shift_y(second, 3, count)
    far = shift_y(left[:part], 1, count), shift_y(right[part:], 3, count)
    second = jnp.concatenate([second, left, *far, right], axis=0)
    for k in range(4):
        if k:
            first = shift_z(first, 1, count)
            second = shift_z(second, 1, count)
        left, right = shift_y(first, 1, count), shift_y(first, 3, count)
        far = shift_y(left[:part], 1, count), shift_y(right[part:], 3, count)
        pieces += [
            (first, [(4 * k, 0, rows, 0, 0)]),
            (left, [(4 * k + 1, 0, rows, 0, 0)]),
            (right, [(4 * k + 3, 0, rows, 0, 0)]),
            (far[0], [(4 * k + 2, 0, part, 0, 0)]),
            (far[1], [(4 * k + 2, 0, part, part, 0)]),
            (second, [(4 * k + j, rows * j, rows, 0, border) for j in range(4)]),
        ]
    return pieces


def on_device(inputs, cotangent, weight, gain):
    sections = lax.axis_size("section")
    count = lax.axis_size("dp")
    half = sections // 2
    section = lax.axis_index("section")
    place = lax.axis_index("dp")
    z, y = place // 4, place % 4
    ahead = jnp.asarray([[z_after(i, k) for i in range(4)] for k in range(4)], jnp.int32)
    behind = jnp.asarray([[z_after(i, -k) for i in range(4)] for k in range(4)], jnp.int32)
    to_z = [ahead[k, z] for k in range(4)]
    from_z = [behind[k, z] for k in range(4)]
    micros, rows, features = inputs.shape
    here = jnp.stack([section, y]).astype(jnp.int32)
    gain_row = lax.dynamic_index_in_dim(gain, section, 0, keepdims=True)
    across = [(i, mirrored(i, count)) for i in range(count)]
    row_of = jnp.stack([from_z[k] * 4 + (y - j) % 4 for k in range(4) for j in range(4)])
    row_of = (row_of * weight.shape[1]).astype(jnp.int32)
    matrix = hold(gather(weight[0], count), row_of, (features, features))
    cotangent, matrix = lax.optimization_barrier((cotangent, matrix))
    upstream = lax.ppermute(cotangent, "dp", across)

    kept = [()] * micros
    current = [inputs] * micros
    after = ()
    turned = None
    for t, m in order(sections, micros):
        if t == half and turned is None:
            turned = turn(matrix)
            after += (turned,)
        result, *kept[m] = forward(t, m, here, current[m], gain_row, matrix, kept[m], after)
        after = (in_hbm(kept[m][0]),)
        current[m] = hop(result, t, half, count) if t + 1 < sections else result

    passed = [()] * micros
    arriving = [upstream] * micros
    normed = [kept[m][1] for m in range(micros)]
    early = exchange(normed, here, 0, EARLY, count)
    after += (in_hbm(early[-1]),)
    for step, m in order(sections, micros):
        t = sections - 1 - step
        result, *passed[m] = backward(
            t, m, here, arriving[m], kept[m][0], kept[m][2], gain_row, turned, passed[m], after
        )
        after = (in_hbm(passed[m][0]),)
        arriving[m] = hop(result, t - 1, half, count) if t else result
    held = lax.optimization_barrier((*normed, after[0]))
    late = exchange(held[:micros], here, EARLY, sections, count)
    normed = [jnp.where(section < EARLY, a, b) for a, b in zip(early, late)]

    slope = jnp.concatenate([passed[m][0] for m in range(micros)], axis=0)
    wide = features // 4
    slope = [
        lax.dynamic_slice_in_dim(slope, to_z[k] * wide, wide, axis=1) for k in range(4)
    ]
    slope = slope[:1] + [shift_z(slope[k], k, count) for k in (1, 2, 3)]
    slope = from_all_y(jnp.concatenate(slope, axis=0), count)
    slope = jnp.stack(slope).reshape(4, 4, micros * rows, features // 4)
    product = jnp.einsum(
        "jkra,kjrb->ab", jnp.stack(normed), slope, preferred_element_type=F32
    ).astype(BF)
    product = product.reshape(4, features // 16, features // 4)
    weight_grad = jnp.zeros((features // 16, features), BF)
    for k in range(4):
        piece = pick(product, to_z[k])
        piece = shift_z(piece, k, count) if k else piece
        at = from_z[k] * (features // 4)
        weight_grad = lax.dynamic_update_slice_in_dim(weight_grad, piece, at, 1)

    total = sum(passed[m][1] for m in range(micros))
    total = total + (shift_y(total, 1, count) + shift_y(total, 2, count) + shift_y(total, 3, count))
    total = total + (shift_z(total, 1, count) + shift_z(total, 2, count) + shift_z(total, 3, count))
    last = lax.ppermute(jnp.concatenate(current, axis=0), "dp", across)
    first_share, final_share = spread(jnp.concatenate(arriving, axis=0), last, sections, section)
    shape = (micros, rows, features // sections)
    return (
        weight_grad[None],
        total,
        first_share.reshape(shape),
        final_share.reshape(shape),
    )


def solution(mesh):
    in_specs = (P(None, "dp", None), P(None, "dp", None), P("section", "dp", None), P())
    out_specs = (
        P("section", "dp", None),
        P("section", None),
        P(None, "dp", "section"),
        P(None, "dp", "section"),
    )
    return jax.shard_map(
        on_device, mesh=mesh, in_specs=in_specs, out_specs=out_specs, check_vma=False
    )
```

```python
import functools

import jax
import jax.numpy as jnp
import numpy as np
from jax import lax
from jax.experimental import pallas as pl
from jax.experimental.pallas import tpu as pltpu
from jax.sharding import PartitionSpec as P

EPSILON = 1e-06
HALF_ROOT = 0.7071067811865476
DENSITY = 0.3989422804014327
BF = jnp.bfloat16
F32 = jnp.float32
ANY = pl.BlockSpec(memory_space=pl.ANY)
HBM = pl.BlockSpec(memory_space=pltpu.HBM)
VMEM = pl.BlockSpec(memory_space=pltpu.VMEM)
SMEM = pl.BlockSpec(memory_space=pltpu.SMEM)
TILE = 512
LIMIT = 8 * 1024 * 1024
EARLY = 8
MICROS = 2


def call(kernel, outs, in_specs, out_specs, aliases, scratch, operands):
    return pl.pallas_call(
        kernel,
        out_shape=outs,
        in_specs=in_specs,
        out_specs=out_specs,
        input_output_aliases=aliases,
        scratch_shapes=scratch,
        compiler_params=pltpu.CompilerParams(vmem_limit_bytes=LIMIT),
        cost_estimate=pl.CostEstimate(flops=1, bytes_accessed=1, transcendentals=0),
    )(*operands)


def hold_kernel(places, row_of, *refs):
    *pieces, held, sems = refs
    copies = []
    for i, (piece, (slot, start, rows, offset, column)) in enumerate(
        (piece, part) for piece, parts in zip(pieces, places) for part in parts
    ):
        row = pl.multiple_of(row_of[slot], 64) + offset
        copies.append(
            pltpu.make_async_copy(
                piece.at[pl.ds(start, rows), :],
                held.at[pl.ds(row, rows), pl.ds(column, piece.shape[1])],
                sems.at[i],
            )
        )
        copies[-1].start()
    for copy in copies:
        copy.wait()


def hold(pieces, row_of, shape):
    arrays, places = zip(*pieces)
    return call(
        functools.partial(hold_kernel, places),
        pltpu.VMEM(shape, BF),
        [SMEM] + [HBM] * len(arrays),
        VMEM,
        {},
        [pltpu.SemaphoreType.DMA((sum(len(p) for p in places),))],
        [row_of] + [in_hbm(array) for array in arrays],
    )


def turn_kernel(source, turned):
    for i in range(0, source.shape[0], TILE):
        for j in range(0, source.shape[1], TILE):
            turned[pl.ds(j, TILE), pl.ds(i, TILE)] = source[pl.ds(i, TILE), pl.ds(j, TILE)].T


def turn(matrix):
    shape = pltpu.VMEM(matrix.shape, matrix.dtype)
    return call(turn_kernel, shape, [VMEM], VMEM, {}, [], [matrix])


def in_hbm(array):
    return pltpu.with_memory_space_constraint(array, pltpu.HBM)


def unit_of(values):
    scale = lax.rsqrt(jnp.mean(values * values, axis=-1, keepdims=True) + EPSILON)
    return scale, values * scale


def forward_kernel(t, m, section, x_in, gain, matrix, *refs):
    y, saved_out, normed_out, factor_out, saved, normed, factor, sems = refs[-8:]

    @pl.when(section[0] == t)
    def _():
        x = x_in.at[m] if m is not None else x_in
        saved[...] = x[...]
        keep = [pltpu.make_async_copy(saved, saved_out, sems.at[0])]
        keep[-1].start()
        _, unit = unit_of(saved[...].astype(F32))
        normed[...] = (unit * gain[...]).astype(BF)
        keep.append(pltpu.make_async_copy(normed, normed_out, sems.at[1]))
        keep[-1].start()
        for n in range(saved.shape[1] // TILE):
            at = pl.ds(n * TILE, TILE)
            pre = jnp.dot(normed[...], matrix[:, at], preferred_element_type=F32)
            bell = 0.5 * (1.0 + lax.erf(pre * HALF_ROOT))
            y[:, at] = (saved[:, at].astype(F32) + pre * bell).astype(BF)
            factor[:, at] = bell + pre * jnp.exp(-0.5 * pre * pre) * DENSITY
            copy = pltpu.make_async_copy(factor.at[:, at], factor_out.at[:, at], sems.at[2 + n])
            copy.start()
            keep.append(copy)
        for copy in keep:
            copy.wait()


def forward(t, m, section, x, gain_row, matrix, kept, after):
    shape = x.shape[-2:]
    wide, deep = pltpu.HBM(shape, BF), pltpu.HBM(shape, F32)
    return call(
        functools.partial(forward_kernel, t, m if x.ndim == 3 else None),
        (pltpu.VMEM(shape, BF), wide, wide, deep),
        [SMEM] + [VMEM] * 3 + [HBM] * len(kept) + [VMEM] * len(after),
        (VMEM, HBM, HBM, HBM),
        {4 + i: 1 + i for i in range(len(kept))},
        [
            pltpu.VMEM(shape, BF),
            pltpu.VMEM(shape, BF),
            pltpu.VMEM(shape, F32),
            pltpu.SemaphoreType.DMA((2 + shape[1] // TILE,)),
        ],
        [section, x, gain_row, matrix, *kept, *after],
    )


def backward_kernel(t, m, section, u_in, saved, factor, gain, turned, *refs):
    d, slope_out, term_out, slope, term, grad, sems = refs[-7:]

    @pl.when(section[0] == t)
    def _():
        u = u_in.at[m] if m is not None else u_in
        slope[...] = (u[...].astype(F32) * factor[...]).astype(BF)
        keep_slope = pltpu.make_async_copy(slope, slope_out, sems.at[0])
        keep_slope.start()
        for k in range(0, saved.shape[1], TILE):
            at = pl.ds(k, TILE)
            grad[:, at] = jnp.dot(slope[...], turned[:, at], preferred_element_type=F32)
        scale, unit = unit_of(saved[...].astype(F32))
        normed_grad = grad[...]
        term[...] = jnp.sum(normed_grad * unit, axis=0, keepdims=True)
        keep_term = pltpu.make_async_copy(term, term_out, sems.at[1])
        keep_term.start()
        unit_grad = normed_grad * gain[...]
        centred = unit_grad - unit * jnp.mean(unit_grad * unit, axis=-1, keepdims=True)
        d[...] = (u[...].astype(F32) + scale * centred).astype(BF)
        keep_slope.wait()
        keep_term.wait()


def backward(t, m, section, u, saved, factor, gain_row, turned, kept, after):
    shape = saved.shape
    return call(
        functools.partial(backward_kernel, t, m if u.ndim == 3 else None),
        (pltpu.VMEM(shape, BF), pltpu.HBM(shape, BF), pltpu.HBM((1, shape[1]), F32)),
        [SMEM] + [VMEM] * 5 + [HBM] * (len(kept) + len(after)),
        (VMEM, HBM, HBM),
        {6 + i: 1 + i for i in range(len(kept))},
        [
            pltpu.VMEM(shape, BF),
            pltpu.VMEM((1, shape[1]), F32),
            pltpu.VMEM(shape, F32),
            pltpu.SemaphoreType.DMA((2,)),
        ],
        [section, u, saved, factor, gain_row, turned, *kept, *after],
    )


def hop(block, lower, half, count):
    if lower % half == half - 1:
        lowers = [lower]
    else:
        lowers = [t for t in range(2 * half) if t % 4 == lower % 4 and t % half != half - 1]
    pairs = []
    for t in lowers:
        for i in range(count):
            near, far = t * count + i, (t + 1) * count + i
            pairs += [(near, far), (far, near)]
    return lax.ppermute(block, ("section", "dp"), sorted(pairs))


def spread(block, sections, section):
    rows = block.shape[0] // 2
    owned = lax.broadcasted_iota(jnp.int32, (2 * rows, 1), 0) >= rows
    bit = sections // 2
    while bit:
        width = block.shape[1] // 2
        low, high = block[:, :width], block[:, width:]
        upper = (section & bit) != 0
        pairs = [(s, s ^ bit) for s in range(sections)]
        arrived = lax.ppermute(jnp.where(upper, low, high), "section", pairs)
        block = jnp.where(owned == upper, jnp.where(upper, high, low), arrived)
        bit //= 2
    return block[:rows], block[rows:]


def cut_kernel(low, high, here, *refs):
    parts, (*out, whole, cut, sems) = refs[:MICROS], refs[-7:]

    @pl.when((here[0] >= low) & (here[0] < high))
    def _():
        rows = parts[0].shape[0]
        loads = [
            pltpu.make_async_copy(part, whole.at[pl.ds(i * rows, rows), :], sems.at[i])
            for i, part in enumerate(parts)
        ]
        for load in loads:
            load.start()
        for load in loads:
            load.wait()
        width = whole.shape[1] // 16
        for y in range(4):

            @pl.when(here[1] == y)
            def _():
                for k in range(4):
                    for z in range(4):
                        column = (4 * z + (y + k) % 4) * width
                        cut[k, :, pl.ds(z * width, width)] = whole[:, pl.ds(column, width)]

        stores = [pltpu.make_async_copy(cut.at[k], out[k], sems.at[k]) for k in range(4)]
        for store in stores:
            store.start()
        for store in stores:
            store.wait()


def cut_columns(parts, here, low, high, after):
    rows, features = MICROS * parts[0].shape[0], parts[0].shape[1]
    return call(
        functools.partial(cut_kernel, low, high),
        tuple(pltpu.HBM((rows, features // 4), BF) for _ in range(4)),
        [SMEM] + [HBM] * (MICROS + len(after)),
        (HBM,) * 4,
        {},
        [
            pltpu.VMEM((rows, features), BF),
            pltpu.VMEM((4, rows, features // 4), BF),
            pltpu.SemaphoreType.DMA((4,)),
        ],
        [here, *(in_hbm(part) for part in (*parts, *after))],
    )


def echo_kernel(here, _after, out):
    out[0] = here[0]
    out[1] = here[1]


def echo(here, after):
    shape = jax.ShapeDtypeStruct(here.shape, here.dtype)
    return call(echo_kernel, shape, [SMEM, HBM], SMEM, {}, [], [here, in_hbm(after)])


def pile_kernel(low, high, here, *refs):
    *parts, out, sems = refs

    @pl.when((here[0] >= low) & (here[0] < high))
    def _():
        copies = [
            pltpu.make_async_copy(part, out.at[k], sems.at[k]) for k, part in enumerate(parts)
        ]
        for copy in copies:
            copy.start()
        for copy in copies:
            copy.wait()


def pile(parts, here, low, high):
    return call(
        functools.partial(pile_kernel, low, high),
        pltpu.HBM((len(parts), *parts[0].shape), BF),
        [SMEM] + [HBM] * len(parts),
        HBM,
        {},
        [pltpu.SemaphoreType.DMA((len(parts),))],
        [here, *(in_hbm(part) for part in parts)],
    )


def exchange(parts, here, low, high, count, after=()):
    sections = range(low, high)
    cut = cut_columns(parts, here, low, high, after)
    pieces = [cut[0]]
    for k in (1, 2, 3):
        pairs = [(s * count + i, s * count + i // 4 * 4 + (i + k) % 4) for s in sections for i in range(count)]
        pieces.append(lax.ppermute(cut[k], ("section", "dp"), pairs))
    blocks = [pile(pieces, here, low, high)]
    pairs = [(s * count + i, s * count + 4 * z_after(i // 4, 1) + i % 4) for s in sections for i in range(count)]
    for _ in range(3):
        blocks.append(lax.ppermute(blocks[-1], ("section", "dp"), pairs))
    return blocks


RING = (0, 2, 3, 1)


def z_after(z, k):
    return RING[(RING.index(z) + k) % len(RING)]


def shift_z(block, k, count):
    pairs = [(i, 4 * z_after(i // 4, k) + i % 4) for i in range(count)]
    return lax.ppermute(block, "dp", pairs)


def shift_y(block, k, count):
    pairs = [(i, i // 4 * 4 + (i + k) % 4) for i in range(count)]
    return lax.ppermute(block, "dp", pairs)


def pick(blocks, at):
    return lax.dynamic_index_in_dim(blocks, at, 0, keepdims=False)


def from_all_y(block, count):
    left, right = shift_y(block, 1, count), shift_y(block, 3, count)
    rows = block.shape[0] // 2
    far = jnp.concatenate(
        [shift_y(left[:rows], 1, count), shift_y(right[rows:], 3, count)], axis=0
    )
    return [block, left, far, right]


def from_all_z(block, count):
    blocks = [block]
    for _ in range(3):
        blocks.append(shift_z(blocks[-1], 1, count))
    return blocks


def gather(shard, count):
    rows, features = shard.shape
    part, border = rows // 2, features * 3 // 4
    pieces = []
    first, second = shard[:, :border], shard[:, border:]
    left, right = shift_y(second, 1, count), shift_y(second, 3, count)
    far = shift_y(left[:part], 1, count), shift_y(right[part:], 3, count)
    second = jnp.concatenate([second, left, *far, right], axis=0)
    for k in range(4):
        if k:
            first = shift_z(first, 1, count)
            second = shift_z(second, 1, count)
        left, right = shift_y(first, 1, count), shift_y(first, 3, count)
        far = shift_y(left[:part], 1, count), shift_y(right[part:], 3, count)
        pieces += [
            (first, [(4 * k, 0, rows, 0, 0)]),
            (left, [(4 * k + 1, 0, rows, 0, 0)]),
            (right, [(4 * k + 3, 0, rows, 0, 0)]),
            (far[0], [(4 * k + 2, 0, part, 0, 0)]),
            (far[1], [(4 * k + 2, 0, part, part, 0)]),
            (second, [(4 * k + j, rows * j, rows, 0, border) for j in range(4)]),
        ]
    return pieces


def on_device(inputs, cotangent, weight, gain):
    sections = lax.axis_size("section")
    count = lax.axis_size("dp")
    half = sections // 2
    section = lax.axis_index("section")
    place = lax.axis_index("dp")
    z, y = place // 4, place % 4
    ahead = jnp.asarray([[z_after(i, k) for i in range(4)] for k in range(4)], jnp.int32)
    behind = jnp.asarray([[z_after(i, -k) for i in range(4)] for k in range(4)], jnp.int32)
    to_z = [ahead[k, z] for k in range(4)]
    from_z = [behind[k, z] for k in range(4)]
    *batches, features = inputs.shape
    micros, rows = MICROS, batches[0] * batches[1] // MICROS
    inputs = inputs.reshape(micros, rows, features)
    cotangent = cotangent.reshape(micros, rows, features)
    here = jnp.stack([section, y]).astype(jnp.int32)
    gain_row = lax.dynamic_index_in_dim(gain, section, 0, keepdims=True)
    row_of = jnp.stack([from_z[k] * 4 + (y - j) % 4 for k in range(4) for j in range(4)])
    row_of = (row_of * weight.shape[1]).astype(jnp.int32)
    matrix = hold(gather(weight[0], count), row_of, (features, features))
    upstream = cotangent

    kept = [()] * micros
    current = [inputs] * micros
    for t in range(sections):
        after = ()
        if t == half:
            turned = turn(matrix)
            after = (turned,)
        for m in range(micros):
            result, *kept[m] = forward(t, m, here, current[m], gain_row, matrix, kept[m], after)
            current[m] = hop(result, t, half, count) if t + 1 < sections else result

    normed = [kept[m][1] for m in range(micros)]
    early = exchange(normed, here, 0, EARLY, count)
    passed = [()] * micros
    arriving = [upstream] * micros
    for t in reversed(range(sections)):
        after = (in_hbm(early[-1]),) if t == sections - 1 else ()
        for m in range(micros):
            result, *passed[m] = backward(
                t, m, here, arriving[m], kept[m][0], kept[m][2], gain_row, turned, passed[m], after
            )
            arriving[m] = hop(result, t - 1, half, count) if t else result
    ended = [passed[m][0] for m in range(micros)]
    late = exchange(normed, here, EARLY, sections, count, ended)
    normed = [jnp.where(section < EARLY, a, b) for a, b in zip(early, late)]

    slope = jnp.concatenate([passed[m][0] for m in range(micros)], axis=0)
    wide = features // 4
    slope = [
        lax.dynamic_slice_in_dim(slope, to_z[k] * wide, wide, axis=1) for k in range(4)
    ]
    slope = slope[:1] + [shift_z(slope[k], k, count) for k in (1, 2, 3)]
    slope = from_all_y(jnp.concatenate(slope, axis=0), count)
    slope = jnp.stack(slope).reshape(4, 4, micros * rows, features // 4)
    product = jnp.einsum(
        "jkra,kjrb->ab", jnp.stack(normed), slope, preferred_element_type=F32
    ).astype(BF)
    product = product.reshape(4, features // 16, features // 4)
    weight_grad = jnp.zeros((features // 16, features), BF)
    for k in range(4):
        piece = pick(product, to_z[k])
        piece = shift_z(piece, k, count) if k else piece
        at = from_z[k] * (features // 4)
        weight_grad = lax.dynamic_update_slice_in_dim(weight_grad, piece, at, 1)

    total = sum(passed[m][1] for m in range(micros))
    total = total + (shift_y(total, 1, count) + shift_y(total, 2, count) + shift_y(total, 3, count))
    total = total + (shift_z(total, 1, count) + shift_z(total, 2, count) + shift_z(total, 3, count))
    ends = pile((*arriving, *current), here, 0, sections).reshape(-1, features)
    first_share, final_share = spread(ends, sections, echo(here, ended[-1])[0])
    shape = (*batches, features // sections)
    return (
        weight_grad[None],
        total,
        first_share.reshape(shape),
        final_share.reshape(shape),
    )


def solution(mesh):
    in_specs = (P(None, "dp", None), P(None, "dp", None), P("section", "dp", None), P())
    out_specs = (
        P("section", "dp", None),
        P("section", None),
        P(None, "dp", "section"),
        P(None, "dp", "section"),
    )
    return jax.shard_map(
        on_device, mesh=mesh, in_specs=in_specs, out_specs=out_specs, check_vma=False
    )
```

```python
import functools

import jax
import jax.numpy as jnp
import numpy as np
from jax import lax
from jax.experimental import pallas as pl
from jax.experimental.pallas import tpu as pltpu
from jax.sharding import PartitionSpec as P

EPSILON = 1e-06
HALF_ROOT = 0.7071067811865476
DENSITY = 0.3989422804014327
BF = jnp.bfloat16
F32 = jnp.float32
ANY = pl.BlockSpec(memory_space=pl.ANY)
HBM = pl.BlockSpec(memory_space=pltpu.HBM)
VMEM = pl.BlockSpec(memory_space=pltpu.VMEM)
SMEM = pl.BlockSpec(memory_space=pltpu.SMEM)
TILE = 512
LIMIT = 8 * 1024 * 1024
EARLY = 8
MICROS = 2


def call(kernel, outs, in_specs, out_specs, aliases, scratch, operands):
    return pl.pallas_call(
        kernel,
        out_shape=outs,
        in_specs=in_specs,
        out_specs=out_specs,
        input_output_aliases=aliases,
        scratch_shapes=scratch,
        compiler_params=pltpu.CompilerParams(vmem_limit_bytes=LIMIT),
        cost_estimate=pl.CostEstimate(flops=1, bytes_accessed=1, transcendentals=0),
    )(*operands)


def hold_kernel(places, row_of, *refs):
    *pieces, held, sems = refs
    copies = []
    for i, (piece, (slot, start, rows, offset, column)) in enumerate(
        (piece, part) for piece, parts in zip(pieces, places) for part in parts
    ):
        row = pl.multiple_of(row_of[slot], 64) + offset
        copies.append(
            pltpu.make_async_copy(
                piece.at[pl.ds(start, rows), :],
                held.at[pl.ds(row, rows), pl.ds(column, piece.shape[1])],
                sems.at[i],
            )
        )
        copies[-1].start()
    for copy in copies:
        copy.wait()


def hold(pieces, row_of, shape):
    arrays, places = zip(*pieces)
    return call(
        functools.partial(hold_kernel, places),
        pltpu.VMEM(shape, BF),
        [SMEM] + [HBM] * len(arrays),
        VMEM,
        {},
        [pltpu.SemaphoreType.DMA((sum(len(p) for p in places),))],
        [row_of] + [in_hbm(array) for array in arrays],
    )


def turn_kernel(source, turned):
    for i in range(0, source.shape[0], TILE):
        for j in range(0, source.shape[1], TILE):
            turned[pl.ds(j, TILE), pl.ds(i, TILE)] = source[pl.ds(i, TILE), pl.ds(j, TILE)].T


def turn(matrix):
    shape = pltpu.VMEM(matrix.shape, matrix.dtype)
    return call(turn_kernel, shape, [VMEM], VMEM, {}, [], [matrix])


def in_hbm(array):
    return pltpu.with_memory_space_constraint(array, pltpu.HBM)


def unit_of(values):
    scale = lax.rsqrt(jnp.mean(values * values, axis=-1, keepdims=True) + EPSILON)
    return scale, values * scale


def forward_kernel(t, m, section, x_in, gain, matrix, *refs):
    y, saved_out, normed_out, factor_out, saved, normed, factor, sems = refs[-8:]

    @pl.when(section[0] == t)
    def _():
        x = x_in.at[m] if m is not None else x_in
        saved[...] = x[...]
        keep = [pltpu.make_async_copy(saved, saved_out, sems.at[0])]
        keep[-1].start()
        _, unit = unit_of(saved[...].astype(F32))
        normed[...] = (unit * gain[...]).astype(BF)
        keep.append(pltpu.make_async_copy(normed, normed_out, sems.at[1]))
        keep[-1].start()
        for n in range(saved.shape[1] // TILE):
            at = pl.ds(n * TILE, TILE)
            pre = jnp.dot(normed[...], matrix[:, at], preferred_element_type=F32)
            bell = 0.5 * (1.0 + lax.erf(pre * HALF_ROOT))
            y[:, at] = (saved[:, at].astype(F32) + pre * bell).astype(BF)
            factor[:, at] = bell + pre * jnp.exp(-0.5 * pre * pre) * DENSITY
            copy = pltpu.make_async_copy(factor.at[:, at], factor_out.at[:, at], sems.at[2 + n])
            copy.start()
            keep.append(copy)
        for copy in keep:
            copy.wait()


def forward(t, m, section, x, gain_row, matrix, kept, after, held):
    shape = x.shape[-2:]
    wide, deep = pltpu.HBM(shape, BF), pltpu.HBM(shape, F32)
    return call(
        functools.partial(forward_kernel, t, m if x.ndim == 3 else None),
        (pltpu.VMEM(shape, BF), wide, wide, deep),
        [SMEM] + [VMEM] * 3 + [HBM] * (len(kept) + len(after)) + [VMEM] * len(held),
        (VMEM, HBM, HBM, HBM),
        {4 + i: 1 + i for i in range(len(kept))},
        [
            pltpu.VMEM(shape, BF),
            pltpu.VMEM(shape, BF),
            pltpu.VMEM(shape, F32),
            pltpu.SemaphoreType.DMA((2 + shape[1] // TILE,)),
        ],
        [section, x, gain_row, matrix, *kept, *after, *held],
    )


def backward_kernel(t, m, section, u_in, saved, factor, gain, turned, *refs):
    d, slope_out, term_out, slope, term, grad, sems = refs[-7:]

    @pl.when(section[0] == t)
    def _():
        u = u_in.at[m] if m is not None else u_in
        slope[...] = (u[...].astype(F32) * factor[...]).astype(BF)
        keep_slope = pltpu.make_async_copy(slope, slope_out, sems.at[0])
        keep_slope.start()
        for k in range(0, saved.shape[1], TILE):
            at = pl.ds(k, TILE)
            grad[:, at] = jnp.dot(slope[...], turned[:, at], preferred_element_type=F32)
        scale, unit = unit_of(saved[...].astype(F32))
        normed_grad = grad[...]
        term[...] = jnp.sum(normed_grad * unit, axis=0, keepdims=True)
        keep_term = pltpu.make_async_copy(term, term_out, sems.at[1])
        keep_term.start()
        unit_grad = normed_grad * gain[...]
        centred = unit_grad - unit * jnp.mean(unit_grad * unit, axis=-1, keepdims=True)
        d[...] = (u[...].astype(F32) + scale * centred).astype(BF)
        keep_slope.wait()
        keep_term.wait()


def backward(t, m, section, u, saved, factor, gain_row, turned, kept, after):
    shape = saved.shape
    return call(
        functools.partial(backward_kernel, t, m if u.ndim == 3 else None),
        (pltpu.VMEM(shape, BF), pltpu.HBM(shape, BF), pltpu.HBM((1, shape[1]), F32)),
        [SMEM] + [VMEM] * 5 + [HBM] * (len(kept) + len(after)),
        (VMEM, HBM, HBM),
        {6 + i: 1 + i for i in range(len(kept))},
        [
            pltpu.VMEM(shape, BF),
            pltpu.VMEM((1, shape[1]), F32),
            pltpu.VMEM(shape, F32),
            pltpu.SemaphoreType.DMA((2,)),
        ],
        [section, u, saved, factor, gain_row, turned, *kept, *after],
    )


def hop(block, lower, half, count):
    if lower % half == half - 1:
        lowers = [lower]
    else:
        lowers = [t for t in range(2 * half) if t % 4 == lower % 4 and t % half != half - 1]
    pairs = []
    for t in lowers:
        for i in range(count):
            near, far = t * count + i, (t + 1) * count + i
            pairs += [(near, far), (far, near)]
    return lax.ppermute(block, ("section", "dp"), sorted(pairs))


def order(sections, micros):
    return [(t + i, m) for t in range(0, sections, 2) for m in range(micros) for i in (0, 1)]


def spread(block, sections, section):
    rows = block.shape[0] // 2
    owned = lax.broadcasted_iota(jnp.int32, (2 * rows, 1), 0) >= rows
    bit = sections // 2
    while bit:
        width = block.shape[1] // 2
        low, high = block[:, :width], block[:, width:]
        upper = (section & bit) != 0
        pairs = [(s, s ^ bit) for s in range(sections)]
        arrived = lax.ppermute(jnp.where(upper, low, high), "section", pairs)
        block = jnp.where(owned == upper, jnp.where(upper, high, low), arrived)
        bit //= 2
    return block[:rows], block[rows:]


def cut_kernel(low, high, here, *refs):
    parts, (*out, whole, cut, sems) = refs[:MICROS], refs[-7:]

    @pl.when((here[0] >= low) & (here[0] < high))
    def _():
        rows = parts[0].shape[0]
        loads = [
            pltpu.make_async_copy(part, whole.at[pl.ds(i * rows, rows), :], sems.at[i])
            for i, part in enumerate(parts)
        ]
        for load in loads:
            load.start()
        for load in loads:
            load.wait()
        width = whole.shape[1] // 16
        for y in range(4):

            @pl.when(here[1] == y)
            def _():
                for k in range(4):
                    for z in range(4):
                        column = (4 * z + (y + k) % 4) * width
                        cut[k, :, pl.ds(z * width, width)] = whole[:, pl.ds(column, width)]

        stores = [pltpu.make_async_copy(cut.at[k], out[k], sems.at[k]) for k in range(4)]
        for store in stores:
            store.start()
        for store in stores:
            store.wait()


def cut_columns(parts, here, low, high, after):
    rows, features = MICROS * parts[0].shape[0], parts[0].shape[1]
    return call(
        functools.partial(cut_kernel, low, high),
        tuple(pltpu.HBM((rows, features // 4), BF) for _ in range(4)),
        [SMEM] + [HBM] * (MICROS + len(after)),
        (HBM,) * 4,
        {},
        [
            pltpu.VMEM((rows, features), BF),
            pltpu.VMEM((4, rows, features // 4), BF),
            pltpu.SemaphoreType.DMA((4,)),
        ],
        [here, *(in_hbm(part) for part in (*parts, *after))],
    )


def pin_kernel(here, *refs):
    for ref in refs:
        if ref.shape == here.shape:
            ref[0] = here[0]
            ref[1] = here[1]


def pin(here, arrays, after):
    return call(
        pin_kernel,
        (
            jax.ShapeDtypeStruct(here.shape, here.dtype),
            *(pltpu.HBM(array.shape, array.dtype) for array in arrays),
        ),
        [SMEM] + [HBM] * (len(arrays) + len(after)),
        (SMEM,) + (HBM,) * len(arrays),
        {1 + i: 1 + i for i in range(len(arrays))},
        [],
        [here, *(in_hbm(array) for array in (*arrays, *after))],
    )


def pile_kernel(low, high, here, *refs):
    *parts, out, sems = refs

    @pl.when((here[0] >= low) & (here[0] < high))
    def _():
        copies = [
            pltpu.make_async_copy(part, out.at[k], sems.at[k]) for k, part in enumerate(parts)
        ]
        for copy in copies:
            copy.start()
        for copy in copies:
            copy.wait()


def pile(parts, here, low, high):
    return call(
        functools.partial(pile_kernel, low, high),
        pltpu.HBM((len(parts), *parts[0].shape), BF),
        [SMEM] + [HBM] * len(parts),
        HBM,
        {},
        [pltpu.SemaphoreType.DMA((len(parts),))],
        [here, *(in_hbm(part) for part in parts)],
    )


def exchange(parts, here, low, high, count, after=()):
    sections = range(low, high)
    cut = cut_columns(parts, here, low, high, after)
    pieces = [cut[0]]
    for k in (1, 2, 3):
        pairs = [(s * count + i, s * count + i // 4 * 4 + (i + k) % 4) for s in sections for i in range(count)]
        pieces.append(lax.ppermute(cut[k], ("section", "dp"), pairs))
    blocks = [pile(pieces, here, low, high)]
    pairs = [(s * count + i, s * count + 4 * z_after(i // 4, 1) + i % 4) for s in sections for i in range(count)]
    for _ in range(3):
        blocks.append(lax.ppermute(blocks[-1], ("section", "dp"), pairs))
    return blocks


RING = (0, 2, 3, 1)


def z_after(z, k):
    return RING[(RING.index(z) + k) % len(RING)]


def shift_z(block, k, count):
    pairs = [(i, 4 * z_after(i // 4, k) + i % 4) for i in range(count)]
    return lax.ppermute(block, "dp", pairs)


def shift_y(block, k, count):
    pairs = [(i, i // 4 * 4 + (i + k) % 4) for i in range(count)]
    return lax.ppermute(block, "dp", pairs)


def pick(blocks, at):
    return lax.dynamic_index_in_dim(blocks, at, 0, keepdims=False)


def from_all_y(block, count):
    left, right = shift_y(block, 1, count), shift_y(block, 3, count)
    rows = block.shape[0] // 2
    far = jnp.concatenate(
        [shift_y(left[:rows], 1, count), shift_y(right[rows:], 3, count)], axis=0
    )
    return [block, left, far, right]


def from_all_z(block, count):
    blocks = [block]
    for _ in range(3):
        blocks.append(shift_z(blocks[-1], 1, count))
    return blocks


def gather(shard, count):
    rows, features = shard.shape
    part, border = rows // 2, features * 3 // 4
    pieces = []
    first, second = shard[:, :border], shard[:, border:]
    left, right = shift_y(second, 1, count), shift_y(second, 3, count)
    far = shift_y(left[:part], 1, count), shift_y(right[part:], 3, count)
    second = jnp.concatenate([second, left, *far, right], axis=0)
    for k in range(4):
        if k:
            first = shift_z(first, 1, count)
            second = shift_z(second, 1, count)
        left, right = shift_y(first, 1, count), shift_y(first, 3, count)
        far = shift_y(left[:part], 1, count), shift_y(right[part:], 3, count)
        pieces += [
            (first, [(4 * k, 0, rows, 0, 0)]),
            (left, [(4 * k + 1, 0, rows, 0, 0)]),
            (right, [(4 * k + 3, 0, rows, 0, 0)]),
            (far[0], [(4 * k + 2, 0, part, 0, 0)]),
            (far[1], [(4 * k + 2, 0, part, part, 0)]),
            (second, [(4 * k + j, rows * j, rows, 0, border) for j in range(4)]),
        ]
    return pieces


def on_device(inputs, cotangent, weight, gain):
    sections = lax.axis_size("section")
    count = lax.axis_size("dp")
    half = sections // 2
    section = lax.axis_index("section")
    place = lax.axis_index("dp")
    z, y = place // 4, place % 4
    ahead = jnp.asarray([[z_after(i, k) for i in range(4)] for k in range(4)], jnp.int32)
    behind = jnp.asarray([[z_after(i, -k) for i in range(4)] for k in range(4)], jnp.int32)
    to_z = [ahead[k, z] for k in range(4)]
    from_z = [behind[k, z] for k in range(4)]
    *batches, features = inputs.shape
    micros, rows = MICROS, batches[0] * batches[1] // MICROS
    inputs = inputs.reshape(micros, rows, features)
    cotangent = cotangent.reshape(micros, rows, features)
    here = jnp.stack([section, y]).astype(jnp.int32)
    gain_row = lax.dynamic_index_in_dim(gain, section, 0, keepdims=True)
    row_of = jnp.stack([from_z[k] * 4 + (y - j) % 4 for k in range(4) for j in range(4)])
    row_of = (row_of * weight.shape[1]).astype(jnp.int32)
    matrix = hold(gather(weight[0], count), row_of, (features, features))
    upstream = cotangent

    kept = [()] * micros
    current = [inputs] * micros
    earlier, held = None, ()
    for t, m in order(sections, micros):
        if t == half and not held:
            turned = turn(matrix)
            held = (turned,)
        after = () if earlier in (None, m) else (in_hbm(kept[earlier][0]),)
        result, *kept[m] = forward(
            t, m, here, current[m], gain_row, matrix, kept[m], after, held if (t, m) == (half, 0) else ()
        )
        current[m] = hop(result, t, half, count) if t + 1 < sections else result
        earlier = m

    normed = [kept[m][1] for m in range(micros)]
    early = exchange(normed, here, 0, EARLY, count)
    passed = [()] * micros
    arriving = [upstream] * micros
    earlier = None
    for step, m in order(sections, micros):
        t = sections - 1 - step
        if step == 0:
            after = (in_hbm(early[-1]),)
        else:
            after = () if earlier == m else (in_hbm(passed[earlier][0]),)
        result, *passed[m] = backward(
            t, m, here, arriving[m], kept[m][0], kept[m][2], gain_row, turned, passed[m], after
        )
        arriving[m] = hop(result, t - 1, half, count) if t else result
        earlier = m
    ended = [passed[m][0] for m in range(micros)]
    late = exchange(normed, here, EARLY, sections, count, ended)
    normed = [jnp.where(section < EARLY, a, b) for a, b in zip(early, late)]

    slope = pile(ended, here, 0, sections).reshape(micros * rows, features)
    wide = features // 4
    slope = [
        lax.dynamic_slice_in_dim(slope, to_z[k] * wide, wide, axis=1) for k in range(4)
    ]
    slope = slope[:1] + [shift_z(slope[k], k, count) for k in (1, 2, 3)]
    behind_slope, *terms = pin(here, [passed[m][1] for m in range(micros)], slope[1:])
    slope = from_all_y(pile(slope, here, 0, sections).reshape(-1, wide), count)
    slope = jnp.stack(slope).reshape(4, 4, micros * rows, features // 4)
    product = jnp.einsum(
        "jkra,kjrb->ab", jnp.stack(normed), slope, preferred_element_type=F32
    ).astype(BF)
    product = product.reshape(4, features // 16, features // 4)
    weight_grad = jnp.zeros((features // 16, features), BF)
    for k in range(4):
        piece = pick(product, to_z[k])
        piece = shift_z(piece, k, count) if k else piece
        at = from_z[k] * (features // 4)
        weight_grad = lax.dynamic_update_slice_in_dim(weight_grad, piece, at, 1)

    total = sum(terms)
    total = total + (shift_y(total, 1, count) + shift_y(total, 2, count) + shift_y(total, 3, count))
    total = total + (shift_z(total, 1, count) + shift_z(total, 2, count) + shift_z(total, 3, count))
    ends = pile((*arriving, *current), here, 0, sections).reshape(-1, features)
    first_share, final_share = spread(ends, sections, behind_slope[0])
    shape = (*batches, features // sections)
    return (
        weight_grad[None],
        total,
        first_share.reshape(shape),
        final_share.reshape(shape),
    )


def solution(mesh):
    in_specs = (P(None, "dp", None), P(None, "dp", None), P("section", "dp", None), P())
    out_specs = (
        P("section", "dp", None),
        P("section", None),
        P(None, "dp", "section"),
        P(None, "dp", "section"),
    )
    return jax.shard_map(
        on_device, mesh=mesh, in_specs=in_specs, out_specs=out_specs, check_vma=False
    )
```

```python
import functools

import jax
import jax.numpy as jnp
import numpy as np
from jax import lax
from jax.experimental import pallas as pl
from jax.experimental.pallas import tpu as pltpu
from jax.sharding import PartitionSpec as P

EPSILON = 1e-06
HALF_ROOT = 0.7071067811865476
DENSITY = 0.3989422804014327
BF = jnp.bfloat16
F32 = jnp.float32
ANY = pl.BlockSpec(memory_space=pl.ANY)
HBM = pl.BlockSpec(memory_space=pltpu.HBM)
VMEM = pl.BlockSpec(memory_space=pltpu.VMEM)
SMEM = pl.BlockSpec(memory_space=pltpu.SMEM)
TILE = 512
LIMIT = 8 * 1024 * 1024
EARLY = 8
MICROS = 2


def call(kernel, outs, in_specs, out_specs, aliases, scratch, operands):
    return pl.pallas_call(
        kernel,
        out_shape=outs,
        in_specs=in_specs,
        out_specs=out_specs,
        input_output_aliases=aliases,
        scratch_shapes=scratch,
        compiler_params=pltpu.CompilerParams(vmem_limit_bytes=LIMIT),
        cost_estimate=pl.CostEstimate(flops=1, bytes_accessed=1, transcendentals=0),
    )(*operands)


def hold_kernel(places, row_of, *refs):
    *pieces, held, sems = refs
    copies = []
    for i, (piece, (slot, start, rows, offset, column)) in enumerate(
        (piece, part) for piece, parts in zip(pieces, places) for part in parts
    ):
        row = pl.multiple_of(row_of[slot], 64) + offset
        copies.append(
            pltpu.make_async_copy(
                piece.at[pl.ds(start, rows), :],
                held.at[pl.ds(row, rows), pl.ds(column, piece.shape[1])],
                sems.at[i],
            )
        )
        copies[-1].start()
    for copy in copies:
        copy.wait()


def hold(pieces, row_of, shape):
    arrays, places = zip(*pieces)
    return call(
        functools.partial(hold_kernel, places),
        pltpu.VMEM(shape, BF),
        [SMEM] + [HBM] * len(arrays),
        VMEM,
        {},
        [pltpu.SemaphoreType.DMA((sum(len(p) for p in places),))],
        [row_of] + [in_hbm(array) for array in arrays],
    )


def turn_kernel(source, turned):
    for i in range(0, source.shape[0], TILE):
        for j in range(0, source.shape[1], TILE):
            turned[pl.ds(j, TILE), pl.ds(i, TILE)] = source[pl.ds(i, TILE), pl.ds(j, TILE)].T


def turn(matrix):
    shape = pltpu.VMEM(matrix.shape, matrix.dtype)
    return call(turn_kernel, shape, [VMEM], VMEM, {}, [], [matrix])


def in_hbm(array):
    return pltpu.with_memory_space_constraint(array, pltpu.HBM)


def unit_of(values):
    scale = lax.rsqrt(jnp.mean(values * values, axis=-1, keepdims=True) + EPSILON)
    return scale, values * scale


def forward_kernel(t, m, section, x_in, gain, matrix, *refs):
    y, saved_out, normed_out, factor_out, saved, normed, factor, sems = refs[-8:]

    @pl.when(section[0] == t)
    def _():
        x = x_in.at[m] if m is not None else x_in
        saved[...] = x[...]
        keep = [pltpu.make_async_copy(saved, saved_out, sems.at[0])]
        keep[-1].start()
        _, unit = unit_of(saved[...].astype(F32))
        normed[...] = (unit * gain[...]).astype(BF)
        keep.append(pltpu.make_async_copy(normed, normed_out, sems.at[1]))
        keep[-1].start()
        for n in range(saved.shape[1] // TILE):
            at = pl.ds(n * TILE, TILE)
            pre = jnp.dot(normed[...], matrix[:, at], preferred_element_type=F32)
            bell = 0.5 * (1.0 + lax.erf(pre * HALF_ROOT))
            y[:, at] = (saved[:, at].astype(F32) + pre * bell).astype(BF)
            factor[:, at] = bell + pre * jnp.exp(-0.5 * pre * pre) * DENSITY
            copy = pltpu.make_async_copy(factor.at[:, at], factor_out.at[:, at], sems.at[2 + n])
            copy.start()
            keep.append(copy)
        for copy in keep:
            copy.wait()


def forward(t, m, section, x, gain_row, matrix, kept, after, held):
    shape = x.shape[-2:]
    wide, deep = pltpu.HBM(shape, BF), pltpu.HBM(shape, F32)
    return call(
        functools.partial(forward_kernel, t, m if x.ndim == 3 else None),
        (pltpu.VMEM(shape, BF), wide, wide, deep),
        [SMEM] + [VMEM] * 3 + [HBM] * (len(kept) + len(after)) + [VMEM] * len(held),
        (VMEM, HBM, HBM, HBM),
        {4 + i: 1 + i for i in range(len(kept))},
        [
            pltpu.VMEM(shape, BF),
            pltpu.VMEM(shape, BF),
            pltpu.VMEM(shape, F32),
            pltpu.SemaphoreType.DMA((2 + shape[1] // TILE,)),
        ],
        [section, x, gain_row, matrix, *kept, *after, *held],
    )


def backward_kernel(t, m, section, u_in, saved, factor, gain, turned, *refs):
    d, slope_out, term_out, slope, term, grad, sems = refs[-7:]

    @pl.when(section[0] == t)
    def _():
        u = u_in.at[m] if m is not None else u_in
        slope[...] = (u[...].astype(F32) * factor[...]).astype(BF)
        keep_slope = pltpu.make_async_copy(slope, slope_out, sems.at[0])
        keep_slope.start()
        for k in range(0, saved.shape[1], TILE):
            at = pl.ds(k, TILE)
            grad[:, at] = jnp.dot(slope[...], turned[:, at], preferred_element_type=F32)
        scale, unit = unit_of(saved[...].astype(F32))
        normed_grad = grad[...]
        term[...] = jnp.sum(normed_grad * unit, axis=0, keepdims=True)
        keep_term = pltpu.make_async_copy(term, term_out, sems.at[1])
        keep_term.start()
        unit_grad = normed_grad * gain[...]
        centred = unit_grad - unit * jnp.mean(unit_grad * unit, axis=-1, keepdims=True)
        d[...] = (u[...].astype(F32) + scale * centred).astype(BF)
        keep_slope.wait()
        keep_term.wait()


def backward(t, m, section, u, saved, factor, gain_row, turned, kept, after):
    shape = saved.shape
    return call(
        functools.partial(backward_kernel, t, m if u.ndim == 3 else None),
        (pltpu.VMEM(shape, BF), pltpu.HBM(shape, BF), pltpu.HBM((1, shape[1]), F32)),
        [SMEM] + [VMEM] * 5 + [HBM] * (len(kept) + len(after)),
        (VMEM, HBM, HBM),
        {6 + i: 1 + i for i in range(len(kept))},
        [
            pltpu.VMEM(shape, BF),
            pltpu.VMEM((1, shape[1]), F32),
            pltpu.VMEM(shape, F32),
            pltpu.SemaphoreType.DMA((2,)),
        ],
        [section, u, saved, factor, gain_row, turned, *kept, *after],
    )


def hop(block, lower, half, count):
    if lower % half == half - 1:
        lowers = [lower]
    else:
        lowers = [t for t in range(2 * half) if t % 4 == lower % 4 and t % half != half - 1]
    pairs = []
    for t in lowers:
        for i in range(count):
            near, far = t * count + i, (t + 1) * count + i
            pairs += [(near, far), (far, near)]
    return lax.ppermute(block, ("section", "dp"), sorted(pairs))


def order(sections, micros):
    return [(t, m) for t in range(sections) for m in range(micros)]


def spread(block, sections, section):
    rows = block.shape[0] // 2
    owned = lax.broadcasted_iota(jnp.int32, (2 * rows, 1), 0) >= rows
    bit = sections // 2
    while bit:
        width = block.shape[1] // 2
        low, high = block[:, :width], block[:, width:]
        upper = (section & bit) != 0
        pairs = [(s, s ^ bit) for s in range(sections)]
        arrived = lax.ppermute(jnp.where(upper, low, high), "section", pairs)
        block = jnp.where(owned == upper, jnp.where(upper, high, low), arrived)
        bit //= 2
    return block[:rows], block[rows:]


def cut_kernel(low, high, here, *refs):
    parts, (*out, whole, cut, sems) = refs[:MICROS], refs[-7:]

    @pl.when((here[0] >= low) & (here[0] < high))
    def _():
        rows = parts[0].shape[0]
        loads = [
            pltpu.make_async_copy(part, whole.at[pl.ds(i * rows, rows), :], sems.at[i])
            for i, part in enumerate(parts)
        ]
        for load in loads:
            load.start()
        for load in loads:
            load.wait()
        width = whole.shape[1] // 16
        for y in range(4):

            @pl.when(here[1] == y)
            def _():
                for k in range(4):
                    for z in range(4):
                        column = (4 * z + (y + k) % 4) * width
                        cut[k, :, pl.ds(z * width, width)] = whole[:, pl.ds(column, width)]

        stores = [pltpu.make_async_copy(cut.at[k], out[k], sems.at[k]) for k in range(4)]
        for store in stores:
            store.start()
        for store in stores:
            store.wait()


def cut_columns(parts, here, low, high, after):
    rows, features = MICROS * parts[0].shape[0], parts[0].shape[1]
    return call(
        functools.partial(cut_kernel, low, high),
        tuple(pltpu.HBM((rows, features // 4), BF) for _ in range(4)),
        [SMEM] + [HBM] * (MICROS + len(after)),
        (HBM,) * 4,
        {},
        [
            pltpu.VMEM((rows, features), BF),
            pltpu.VMEM((4, rows, features // 4), BF),
            pltpu.SemaphoreType.DMA((4,)),
        ],
        [here, *(in_hbm(part) for part in (*parts, *after))],
    )


def pin_kernel(here, *refs):
    for ref in refs:
        if ref.shape == here.shape:
            ref[0] = here[0]
            ref[1] = here[1]


def pin(here, arrays, after):
    return call(
        pin_kernel,
        (
            jax.ShapeDtypeStruct(here.shape, here.dtype),
            *(pltpu.HBM(array.shape, array.dtype) for array in arrays),
        ),
        [SMEM] + [HBM] * (len(arrays) + len(after)),
        (SMEM,) + (HBM,) * len(arrays),
        {1 + i: 1 + i for i in range(len(arrays))},
        [],
        [here, *(in_hbm(array) for array in (*arrays, *after))],
    )


def pile_kernel(low, high, here, *refs):
    *parts, out, held, sems = refs

    @pl.when((here[0] >= low) & (here[0] < high))
    def _():
        copies = [
            pltpu.make_async_copy(part, held.at[k], sems.at[k]) for k, part in enumerate(parts)
        ]
        for copy in copies:
            copy.start()
        for copy in copies:
            copy.wait()
        store = pltpu.make_async_copy(held, out, sems.at[0])
        store.start()
        store.wait()


def pile(parts, here, low, high):
    shape = (len(parts), *parts[0].shape)
    return call(
        functools.partial(pile_kernel, low, high),
        pltpu.HBM(shape, BF),
        [SMEM] + [HBM] * len(parts),
        HBM,
        {},
        [pltpu.VMEM(shape, BF), pltpu.SemaphoreType.DMA((len(parts),))],
        [here, *(in_hbm(part) for part in parts)],
    )


def exchange(parts, here, low, high, count, after=()):
    sections = range(low, high)
    cut = cut_columns(parts, here, low, high, after)
    pieces = [cut[0]]
    for k in (1, 2, 3):
        pairs = [(s * count + i, s * count + i // 4 * 4 + (i + k) % 4) for s in sections for i in range(count)]
        pieces.append(lax.ppermute(cut[k], ("section", "dp"), pairs))
    blocks = [pile(pieces, here, low, high)]
    pairs = [(s * count + i, s * count + 4 * z_after(i // 4, 1) + i % 4) for s in sections for i in range(count)]
    for _ in range(3):
        blocks.append(lax.ppermute(blocks[-1], ("section", "dp"), pairs))
    return blocks


RING = (0, 2, 3, 1)


def z_after(z, k):
    return RING[(RING.index(z) + k) % len(RING)]


def shift_z(block, k, count):
    pairs = [(i, 4 * z_after(i // 4, k) + i % 4) for i in range(count)]
    return lax.ppermute(block, "dp", pairs)


def shift_y(block, k, count):
    pairs = [(i, i // 4 * 4 + (i + k) % 4) for i in range(count)]
    return lax.ppermute(block, "dp", pairs)


def pick(blocks, at):
    return lax.dynamic_index_in_dim(blocks, at, 0, keepdims=False)


def from_all_y(block, count):
    left, right = shift_y(block, 1, count), shift_y(block, 3, count)
    rows = block.shape[0] // 2
    far = jnp.concatenate(
        [shift_y(left[:rows], 1, count), shift_y(right[rows:], 3, count)], axis=0
    )
    return [block, left, far, right]


def from_all_z(block, count):
    blocks = [block]
    for _ in range(3):
        blocks.append(shift_z(blocks[-1], 1, count))
    return blocks


def gather(shard, count):
    rows, features = shard.shape
    part, border = rows // 2, features * 3 // 4
    pieces = []
    first, second = shard[:, :border], shard[:, border:]
    left, right = shift_y(second, 1, count), shift_y(second, 3, count)
    far = shift_y(left[:part], 1, count), shift_y(right[part:], 3, count)
    second = jnp.concatenate([second, left, *far, right], axis=0)
    for k in range(4):
        if k:
            first = shift_z(first, 1, count)
            second = shift_z(second, 1, count)
        left, right = shift_y(first, 1, count), shift_y(first, 3, count)
        far = shift_y(left[:part], 1, count), shift_y(right[part:], 3, count)
        pieces += [
            (first, [(4 * k, 0, rows, 0, 0)]),
            (left, [(4 * k + 1, 0, rows, 0, 0)]),
            (right, [(4 * k + 3, 0, rows, 0, 0)]),
            (far[0], [(4 * k + 2, 0, part, 0, 0)]),
            (far[1], [(4 * k + 2, 0, part, part, 0)]),
            (second, [(4 * k + j, rows * j, rows, 0, border) for j in range(4)]),
        ]
    return pieces


def on_device(inputs, cotangent, weight, gain):
    sections = lax.axis_size("section")
    count = lax.axis_size("dp")
    half = sections // 2
    section = lax.axis_index("section")
    place = lax.axis_index("dp")
    z, y = place // 4, place % 4
    ahead = jnp.asarray([[z_after(i, k) for i in range(4)] for k in range(4)], jnp.int32)
    behind = jnp.asarray([[z_after(i, -k) for i in range(4)] for k in range(4)], jnp.int32)
    to_z = [ahead[k, z] for k in range(4)]
    from_z = [behind[k, z] for k in range(4)]
    *batches, features = inputs.shape
    micros, rows = MICROS, batches[0] * batches[1] // MICROS
    inputs = inputs.reshape(micros, rows, features)
    cotangent = cotangent.reshape(micros, rows, features)
    here = jnp.stack([section, y]).astype(jnp.int32)
    gain_row = lax.dynamic_index_in_dim(gain, section, 0, keepdims=True)
    row_of = jnp.stack([from_z[k] * 4 + (y - j) % 4 for k in range(4) for j in range(4)])
    row_of = (row_of * weight.shape[1]).astype(jnp.int32)
    matrix = hold(gather(weight[0], count), row_of, (features, features))
    upstream = cotangent

    kept = [()] * micros
    current = [inputs] * micros
    held = ()
    for t, m in order(sections, micros):
        if t == half and not held:
            turned = turn(matrix)
            held = (turned,)
        result, *kept[m] = forward(
            t, m, here, current[m], gain_row, matrix, kept[m], (), held if (t, m) == (half, 0) else ()
        )
        current[m] = hop(result, t, half, count) if t + 1 < sections else result

    normed = [kept[m][1] for m in range(micros)]
    early = exchange(normed, here, 0, EARLY, count)
    passed = [()] * micros
    arriving = [upstream] * micros
    for step, m in order(sections, micros):
        t = sections - 1 - step
        after = () if step else (in_hbm(early[-1]),)
        result, *passed[m] = backward(
            t, m, here, arriving[m], kept[m][0], kept[m][2], gain_row, turned, passed[m], after
        )
        arriving[m] = hop(result, t - 1, half, count) if t else result
    ended = [passed[m][0] for m in range(micros)]
    late = exchange(normed, here, EARLY, sections, count, ended)
    normed = [jnp.where(section < EARLY, a, b) for a, b in zip(early, late)]

    slope = pile(ended, here, 0, sections).reshape(micros * rows, features)
    wide = features // 4
    slope = [
        lax.dynamic_slice_in_dim(slope, to_z[k] * wide, wide, axis=1) for k in range(4)
    ]
    slope = slope[:1] + [shift_z(slope[k], k, count) for k in (1, 2, 3)]
    behind_slope, *terms = pin(here, [passed[m][1] for m in range(micros)], slope[1:])
    slope = from_all_y(pile(slope, here, 0, sections).reshape(-1, wide), count)
    slope = jnp.stack(slope).reshape(4, 4, micros * rows, features // 4)
    product = jnp.einsum(
        "jkra,kjrb->ab", jnp.stack(normed), slope, preferred_element_type=F32
    ).astype(BF)
    product = product.reshape(4, features // 16, features // 4)
    weight_grad = jnp.zeros((features // 16, features), BF)
    for k in range(4):
        piece = pick(product, to_z[k])
        piece = shift_z(piece, k, count) if k else piece
        at = from_z[k] * (features // 4)
        weight_grad = lax.dynamic_update_slice_in_dim(weight_grad, piece, at, 1)

    total = sum(terms)
    total = total + (shift_y(total, 1, count) + shift_y(total, 2, count) + shift_y(total, 3, count))
    total = total + (shift_z(total, 1, count) + shift_z(total, 2, count) + shift_z(total, 3, count))
    ends = pile((*arriving, *current), here, 0, sections).reshape(-1, features)
    first_share, final_share = spread(ends, sections, behind_slope[0])
    shape = (*batches, features // sections)
    return (
        weight_grad[None],
        total,
        first_share.reshape(shape),
        final_share.reshape(shape),
    )


def solution(mesh):
    in_specs = (P(None, "dp", None), P(None, "dp", None), P("section", "dp", None), P())
    out_specs = (
        P("section", "dp", None),
        P("section", None),
        P(None, "dp", "section"),
        P(None, "dp", "section"),
    )
    return jax.shard_map(
        on_device, mesh=mesh, in_specs=in_specs, out_specs=out_specs, check_vma=False
    )
```

```python
import functools

import jax
import jax.numpy as jnp
import numpy as np
from jax import lax
from jax.experimental import pallas as pl
from jax.experimental.pallas import tpu as pltpu
from jax.sharding import PartitionSpec as P

EPSILON = 1e-06
HALF_ROOT = 0.7071067811865476
DENSITY = 0.3989422804014327
BF = jnp.bfloat16
F32 = jnp.float32
ANY = pl.BlockSpec(memory_space=pl.ANY)
HBM = pl.BlockSpec(memory_space=pltpu.HBM)
VMEM = pl.BlockSpec(memory_space=pltpu.VMEM)
SMEM = pl.BlockSpec(memory_space=pltpu.SMEM)
TILE = 512
LIMIT = 8 * 1024 * 1024
EARLY = 8
MICROS = 2


def call(kernel, outs, in_specs, out_specs, aliases, scratch, operands):
    return pl.pallas_call(
        kernel,
        out_shape=outs,
        in_specs=in_specs,
        out_specs=out_specs,
        input_output_aliases=aliases,
        scratch_shapes=scratch,
        compiler_params=pltpu.CompilerParams(vmem_limit_bytes=LIMIT),
        cost_estimate=pl.CostEstimate(flops=1, bytes_accessed=1, transcendentals=0),
    )(*operands)


def hold_kernel(places, row_of, *refs):
    *pieces, held, sems = refs
    copies = []
    for i, (piece, (slot, start, rows, offset, column)) in enumerate(
        (piece, part) for piece, parts in zip(pieces, places) for part in parts
    ):
        row = pl.multiple_of(row_of[slot], 64) + offset
        copies.append(
            pltpu.make_async_copy(
                piece.at[pl.ds(start, rows), :],
                held.at[pl.ds(row, rows), pl.ds(column, piece.shape[1])],
                sems.at[i],
            )
        )
        copies[-1].start()
    for copy in copies:
        copy.wait()


def hold(pieces, row_of, shape):
    arrays, places = zip(*pieces)
    return call(
        functools.partial(hold_kernel, places),
        pltpu.VMEM(shape, BF),
        [SMEM] + [HBM] * len(arrays),
        VMEM,
        {},
        [pltpu.SemaphoreType.DMA((sum(len(p) for p in places),))],
        [row_of] + [in_hbm(array) for array in arrays],
    )


def turn_kernel(source, turned):
    for i in range(0, source.shape[0], TILE):
        for j in range(0, source.shape[1], TILE):
            turned[pl.ds(j, TILE), pl.ds(i, TILE)] = source[pl.ds(i, TILE), pl.ds(j, TILE)].T


def turn(matrix):
    shape = pltpu.VMEM(matrix.shape, matrix.dtype)
    return call(turn_kernel, shape, [VMEM], VMEM, {}, [], [matrix])


def in_hbm(array):
    return pltpu.with_memory_space_constraint(array, pltpu.HBM)


def unit_of(values):
    scale = lax.rsqrt(jnp.mean(values * values, axis=-1, keepdims=True) + EPSILON)
    return scale, values * scale


def forward_kernel(t, m, section, x_in, gain, matrix, *refs):
    y, saved_out, normed_out, factor_out, saved, normed, factor, sems = refs[-8:]

    @pl.when(section[0] == t)
    def _():
        x = x_in.at[m] if m is not None else x_in
        saved[...] = x[...]
        keep = [pltpu.make_async_copy(saved, saved_out, sems.at[0])]
        keep[-1].start()
        _, unit = unit_of(saved[...].astype(F32))
        normed[...] = (unit * gain[...]).astype(BF)
        keep.append(pltpu.make_async_copy(normed, normed_out, sems.at[1]))
        keep[-1].start()
        for n in range(saved.shape[1] // TILE):
            at = pl.ds(n * TILE, TILE)
            pre = jnp.dot(normed[...], matrix[:, at], preferred_element_type=F32)
            bell = 0.5 * (1.0 + lax.erf(pre * HALF_ROOT))
            y[:, at] = (saved[:, at].astype(F32) + pre * bell).astype(BF)
            factor[:, at] = bell + pre * jnp.exp(-0.5 * pre * pre) * DENSITY
            copy = pltpu.make_async_copy(factor.at[:, at], factor_out.at[:, at], sems.at[2 + n])
            copy.start()
            keep.append(copy)
        for copy in keep:
            copy.wait()


def forward(t, m, section, x, gain_row, matrix, kept, after, held):
    shape = x.shape[-2:]
    wide, deep = pltpu.HBM(shape, BF), pltpu.HBM(shape, F32)
    return call(
        functools.partial(forward_kernel, t, m if x.ndim == 3 else None),
        (pltpu.VMEM(shape, BF), wide, wide, deep),
        [SMEM] + [VMEM] * 3 + [HBM] * (len(kept) + len(after)) + [VMEM] * len(held),
        (VMEM, HBM, HBM, HBM),
        {4 + i: 1 + i for i in range(len(kept))},
        [
            pltpu.VMEM(shape, BF),
            pltpu.VMEM(shape, BF),
            pltpu.VMEM(shape, F32),
            pltpu.SemaphoreType.DMA((2 + shape[1] // TILE,)),
        ],
        [section, x, gain_row, matrix, *kept, *after, *held],
    )


def backward_kernel(t, m, section, u_in, saved, factor, gain, turned, *refs):
    d, slope_out, term_out, slope, term, grad, sems = refs[-7:]

    @pl.when(section[0] == t)
    def _():
        u = u_in.at[m] if m is not None else u_in
        slope[...] = (u[...].astype(F32) * factor[...]).astype(BF)
        keep_slope = pltpu.make_async_copy(slope, slope_out, sems.at[0])
        keep_slope.start()
        for k in range(0, saved.shape[1], TILE):
            at = pl.ds(k, TILE)
            grad[:, at] = jnp.dot(slope[...], turned[:, at], preferred_element_type=F32)
        scale, unit = unit_of(saved[...].astype(F32))
        normed_grad = grad[...]
        term[...] = jnp.sum(normed_grad * unit, axis=0, keepdims=True)
        keep_term = pltpu.make_async_copy(term, term_out, sems.at[1])
        keep_term.start()
        unit_grad = normed_grad * gain[...]
        centred = unit_grad - unit * jnp.mean(unit_grad * unit, axis=-1, keepdims=True)
        d[...] = (u[...].astype(F32) + scale * centred).astype(BF)
        keep_slope.wait()
        keep_term.wait()


def backward(t, m, section, u, saved, factor, gain_row, turned, kept, after):
    shape = saved.shape
    return call(
        functools.partial(backward_kernel, t, m if u.ndim == 3 else None),
        (pltpu.VMEM(shape, BF), pltpu.HBM(shape, BF), pltpu.HBM((1, shape[1]), F32)),
        [SMEM] + [VMEM] * 5 + [HBM] * (len(kept) + len(after)),
        (VMEM, HBM, HBM),
        {6 + i: 1 + i for i in range(len(kept))},
        [
            pltpu.VMEM(shape, BF),
            pltpu.VMEM((1, shape[1]), F32),
            pltpu.VMEM(shape, F32),
            pltpu.SemaphoreType.DMA((2,)),
        ],
        [section, u, saved, factor, gain_row, turned, *kept, *after],
    )


def hop(block, lower, half, count):
    if lower % half == half - 1:
        lowers = [lower]
    else:
        lowers = [t for t in range(2 * half) if t % 4 == lower % 4 and t % half != half - 1]
    pairs = []
    for t in lowers:
        for i in range(count):
            near, far = t * count + i, (t + 1) * count + i
            pairs += [(near, far), (far, near)]
    return lax.ppermute(block, ("section", "dp"), sorted(pairs))


def order(sections, micros):
    return [(t, m) for t in range(sections) for m in range(micros)]


def spread(block, sections, section):
    rows = block.shape[0] // 2
    owned = lax.broadcasted_iota(jnp.int32, (2 * rows, 1), 0) >= rows
    bit = sections // 2
    while bit:
        width = block.shape[1] // 2
        low, high = block[:, :width], block[:, width:]
        upper = (section & bit) != 0
        pairs = [(s, s ^ bit) for s in range(sections)]
        arrived = lax.ppermute(jnp.where(upper, low, high), "section", pairs)
        block = jnp.where(owned == upper, jnp.where(upper, high, low), arrived)
        bit //= 2
    return block[:rows], block[rows:]


def cut_kernel(low, high, here, *refs):
    parts, (*out, whole, cut, sems) = refs[:MICROS], refs[-7:]

    @pl.when((here[0] >= low) & (here[0] < high))
    def _():
        rows = parts[0].shape[0]
        loads = [
            pltpu.make_async_copy(part, whole.at[pl.ds(i * rows, rows), :], sems.at[i])
            for i, part in enumerate(parts)
        ]
        for load in loads:
            load.start()
        for load in loads:
            load.wait()
        width = whole.shape[1] // 16
        for y in range(4):

            @pl.when(here[1] == y)
            def _():
                for k in range(4):
                    for z in range(4):
                        column = (4 * z + (y + k) % 4) * width
                        cut[k, :, pl.ds(z * width, width)] = whole[:, pl.ds(column, width)]

        stores = [pltpu.make_async_copy(cut.at[k], out[k], sems.at[k]) for k in range(4)]
        for store in stores:
            store.start()
        for store in stores:
            store.wait()


def cut_columns(parts, here, low, high, after):
    rows, features = MICROS * parts[0].shape[0], parts[0].shape[1]
    return call(
        functools.partial(cut_kernel, low, high),
        tuple(pltpu.HBM((rows, features // 4), BF) for _ in range(4)),
        [SMEM] + [HBM] * (MICROS + len(after)),
        (HBM,) * 4,
        {},
        [
            pltpu.VMEM((rows, features), BF),
            pltpu.VMEM((4, rows, features // 4), BF),
            pltpu.SemaphoreType.DMA((4,)),
        ],
        [here, *(in_hbm(part) for part in (*parts, *after))],
    )


def pin_kernel(here, *refs):
    for ref in refs:
        if ref.shape == here.shape:
            ref[0] = here[0]
            ref[1] = here[1]


def pin(here, arrays, after):
    return call(
        pin_kernel,
        (
            jax.ShapeDtypeStruct(here.shape, here.dtype),
            *(pltpu.HBM(array.shape, array.dtype) for array in arrays),
        ),
        [SMEM] + [HBM] * (len(arrays) + len(after)),
        (SMEM,) + (HBM,) * len(arrays),
        {1 + i: 1 + i for i in range(len(arrays))},
        [],
        [here, *(in_hbm(array) for array in (*arrays, *after))],
    )


def pile_kernel(low, high, here, *refs):
    *parts, out, held, sems = refs

    @pl.when((here[0] >= low) & (here[0] < high))
    def _():
        copies = [
            pltpu.make_async_copy(part, held.at[k], sems.at[k]) for k, part in enumerate(parts)
        ]
        for copy in copies:
            copy.start()
        for copy in copies:
            copy.wait()
        store = pltpu.make_async_copy(held, out, sems.at[0])
        store.start()
        store.wait()


def pile(parts, here, low, high):
    shape = (len(parts), *parts[0].shape)
    return call(
        functools.partial(pile_kernel, low, high),
        pltpu.HBM(shape, BF),
        [SMEM] + [HBM] * len(parts),
        HBM,
        {},
        [pltpu.VMEM(shape, BF), pltpu.SemaphoreType.DMA((len(parts),))],
        [here, *(in_hbm(part) for part in parts)],
    )


def exchange(parts, here, low, high, count, after=()):
    sections = range(low, high)
    cut = cut_columns(parts, here, low, high, after)
    pieces = [cut[0]]
    for k in (1, 2, 3):
        pairs = [(s * count + i, s * count + i // 4 * 4 + (i + k) % 4) for s in sections for i in range(count)]
        pieces.append(lax.ppermute(cut[k], ("section", "dp"), pairs))
    blocks = [pile(pieces, here, low, high)]
    pairs = [(s * count + i, s * count + 4 * z_after(i // 4, 1) + i % 4) for s in sections for i in range(count)]
    for _ in range(3):
        blocks.append(lax.ppermute(blocks[-1], ("section", "dp"), pairs))
    return blocks


RING = (0, 2, 3, 1)


def z_after(z, k):
    return RING[(RING.index(z) + k) % len(RING)]


def shift_z(block, k, count):
    pairs = [(i, 4 * z_after(i // 4, k) + i % 4) for i in range(count)]
    return lax.ppermute(block, "dp", pairs)


def shift_y(block, k, count):
    pairs = [(i, i // 4 * 4 + (i + k) % 4) for i in range(count)]
    return lax.ppermute(block, "dp", pairs)


def pick(blocks, at):
    return lax.dynamic_index_in_dim(blocks, at, 0, keepdims=False)


def from_all_y(block, count):
    left, right = shift_y(block, 1, count), shift_y(block, 3, count)
    rows = block.shape[0] // 2
    far = jnp.concatenate(
        [shift_y(left[:rows], 1, count), shift_y(right[rows:], 3, count)], axis=0
    )
    return [block, left, far, right]


def from_all_z(block, count):
    blocks = [block]
    for _ in range(3):
        blocks.append(shift_z(blocks[-1], 1, count))
    return blocks


def gather(shard, count):
    rows, features = shard.shape
    part, border = rows // 2, features * 3 // 4
    pieces = []
    first, second = shard[:, :border], shard[:, border:]
    left, right = shift_y(second, 1, count), shift_y(second, 3, count)
    far = shift_y(left[:part], 1, count), shift_y(right[part:], 3, count)
    second = jnp.concatenate([second, left, *far, right], axis=0)
    for k in range(4):
        if k:
            first = shift_z(first, 1, count)
            second = shift_z(second, 1, count)
        left, right = shift_y(first, 1, count), shift_y(first, 3, count)
        far = shift_y(left[:part], 1, count), shift_y(right[part:], 3, count)
        pieces += [
            (first, [(4 * k, 0, rows, 0, 0)]),
            (left, [(4 * k + 1, 0, rows, 0, 0)]),
            (right, [(4 * k + 3, 0, rows, 0, 0)]),
            (far[0], [(4 * k + 2, 0, part, 0, 0)]),
            (far[1], [(4 * k + 2, 0, part, part, 0)]),
            (second, [(4 * k + j, rows * j, rows, 0, border) for j in range(4)]),
        ]
    return pieces


def on_device(inputs, cotangent, weight, gain):
    sections = lax.axis_size("section")
    count = lax.axis_size("dp")
    half = sections // 2
    section = lax.axis_index("section")
    place = lax.axis_index("dp")
    z, y = place // 4, place % 4
    ahead = jnp.asarray([[z_after(i, k) for i in range(4)] for k in range(4)], jnp.int32)
    behind = jnp.asarray([[z_after(i, -k) for i in range(4)] for k in range(4)], jnp.int32)
    to_z = [ahead[k, z] for k in range(4)]
    from_z = [behind[k, z] for k in range(4)]
    *batches, features = inputs.shape
    micros, rows = MICROS, batches[0] * batches[1] // MICROS
    inputs = inputs.reshape(micros, rows, features)
    cotangent = cotangent.reshape(micros, rows, features)
    here = jnp.stack([section, y]).astype(jnp.int32)
    gain_row = lax.dynamic_index_in_dim(gain, section, 0, keepdims=True)
    row_of = jnp.stack([from_z[k] * 4 + (y - j) % 4 for k in range(4) for j in range(4)])
    row_of = (row_of * weight.shape[1]).astype(jnp.int32)
    matrix = hold(gather(weight[0], count), row_of, (features, features))
    upstream = cotangent

    kept = [()] * micros
    current = [inputs] * micros
    held = ()
    for t, m in order(sections, micros):
        if t == half and not held:
            turned = turn(matrix)
            held = (turned,)
        result, *kept[m] = forward(
            t, m, here, current[m], gain_row, matrix, kept[m], (), held if (t, m) == (half, 0) else ()
        )
        current[m] = hop(result, t, half, count) if t + 1 < sections else result

    normed = [kept[m][1] for m in range(micros)]
    early = exchange(normed, here, 0, EARLY, count)
    passed = [()] * micros
    arriving = [upstream] * micros
    for step, m in order(sections, micros):
        t = sections - 1 - step
        after = () if step else (in_hbm(early[-1]),)
        result, *passed[m] = backward(
            t, m, here, arriving[m], kept[m][0], kept[m][2], gain_row, turned, passed[m], after
        )
        arriving[m] = hop(result, t - 1, half, count) if t else result
    ended = [passed[m][0] for m in range(micros)]
    late = exchange(normed, here, EARLY, sections, count, ended)
    normed = [jnp.where(section < EARLY, a, b) for a, b in zip(early, late)]

    slope = pile(ended, here, 0, sections).reshape(micros * rows, features)
    wide = features // 4
    slope = [
        lax.dynamic_slice_in_dim(slope, to_z[k] * wide, wide, axis=1) for k in range(4)
    ]
    slope = slope[:1] + [shift_z(slope[k], k, count) for k in (1, 2, 3)]
    behind_slope, *terms = pin(here, [passed[m][1] for m in range(micros)], (*slope[1:], late[-1]))
    slope = from_all_y(pile(slope, here, 0, sections).reshape(-1, wide), count)
    slope = jnp.stack(slope).reshape(4, 4, micros * rows, features // 4)
    product = jnp.einsum(
        "jkra,kjrb->ab", jnp.stack(normed), slope, preferred_element_type=F32
    ).astype(BF)
    product = product.reshape(4, features // 16, features // 4)
    weight_grad = jnp.zeros((features // 16, features), BF)
    for k in range(4):
        piece = pick(product, to_z[k])
        piece = shift_z(piece, k, count) if k else piece
        at = from_z[k] * (features // 4)
        weight_grad = lax.dynamic_update_slice_in_dim(weight_grad, piece, at, 1)

    total = sum(terms)
    total = total + (shift_y(total, 1, count) + shift_y(total, 2, count) + shift_y(total, 3, count))
    total = total + (shift_z(total, 1, count) + shift_z(total, 2, count) + shift_z(total, 3, count))
    ends = pile((*arriving, *current), here, 0, sections).reshape(-1, features)
    first_share, final_share = spread(ends, sections, behind_slope[0])
    shape = (*batches, features // sections)
    return (
        weight_grad[None],
        total,
        first_share.reshape(shape),
        final_share.reshape(shape),
    )


def solution(mesh):
    in_specs = (P(None, "dp", None), P(None, "dp", None), P("section", "dp", None), P())
    out_specs = (
        P("section", "dp", None),
        P("section", None),
        P(None, "dp", "section"),
        P(None, "dp", "section"),
    )
    return jax.shard_map(
        on_device, mesh=mesh, in_specs=in_specs, out_specs=out_specs, check_vma=False
    )
```
